32 devices in a mesh: axial: 8 (over z, core), circ: 4 (over y, x).
Axes of the slice: x: 2, y: 2, z: 4, core: 2. Of those that a mesh axis runs over, the one named last changes fastest.
Arguments:
- load_terms: float32 [8, 4, 128, 512], P('axial', 'circ'), may hold values from -19 to 19
- diffusivity: float32 [8, 4, 512], P('axial', 'circ'), may hold values from 0.1 to 10
- interface_diag: float32 [8, 4, 512], P('axial', 'circ'), may hold values from 4 to 8
- coupling: float32 [8, 4, 512, 512], P('axial', 'circ'), may hold values from -0.125 to 0.125
- interior_inverse: float32 [8, 4, 4, 128, 128], P('axial', 'circ'), may hold values from -1 to 3, as said below
- neumann_solve: float32 [8, 4, 512, 512], P('axial', 'circ'), may hold values from -1 to 3, as said below
- row_coarse: float32 [8, 8, 8], P('axial'), may hold values from -1 to 3, as said below
- lower_coef: float32 [8, 8], P('axial'), may hold values from 0.1 to 1
- upper_coef: float32 [8, 8], P('axial'), may hold values from 0.1 to 1
- face_order: int32 [8, 4, 512], P('axial', 'circ'), may hold values from 0 to 511, as said below
- primal_lists: int32 [8, 4, 8, 64], P('axial', 'circ'), may hold values from 0 to 511, as said below
Outputs:
- solution_field: float32 [8, 4, 128, 512], P('axial', 'circ')
- residual: float32 [8, 4, 128, 512], P('axial', 'circ')
The draws below stay inside these ranges and needn't reach their ends.
Inputs may be any that keep to these rules, and one draw needn't show every extreme that they name: `face_order`: in each subdomain the values on face f (points f * 128 to f * 128 + 127) are those same numbers in some order; equal values on the two sides of a face name the same point. `primal_lists`: lists 2f and 2f + 1 together name every point of face f once. `interior_inverse`: symmetric in the last two dimensions. `neumann_solve`: symmetric in the last two dimensions. `row_coarse`: Symmetric, each diagonal entry larger than the sum of its row's other magnitudes.
All inputs are finite; a program needn't handle non-finite values.
Results may differ from the reference program's by a relative error of at most 0.0003.
Values sent between devices are 32-bit elements; how exact they have to be, the bound alone decides.
A program may use at most 64 MiB of HBM per device.

```python
import math
import jax
import jax.numpy as jnp
from jax import lax

R = 128
F = 128
NB = 4
BLK = 128
NP = 8
ITERS = 3
SUBDOMAIN_AXIAL = 8
SUB_CI = 4
B = 512
NI = 512
LIST = 64


def symmetric_table(key, count, size, low, high, spread):
    diag_key, off_key = jax.random.split(key)
    diagonal = jax.random.uniform(diag_key, (count, size), jnp.float32, low, high)
    raw = jax.random.uniform(off_key, (count, size, size), jnp.float32, -spread, spread)
    mirrored = 0.5 * (raw + jnp.swapaxes(raw, 1, 2))
    identity = jnp.eye(size, dtype=jnp.float32)[None]
    return mirrored * (1.0 - identity) + identity * diagonal[:, :, None]


def draw_load_terms(key, part):
    base = jnp.clip(jax.random.normal(key, (SUBDOMAIN_AXIAL, SUB_CI, R, B), jnp.float32), -6.0, 6.0)
    rise = 1.0 + 2.0 * jnp.arange(SUBDOMAIN_AXIAL, dtype=jnp.float32) / (SUBDOMAIN_AXIAL - 1)
    return base * rise[:, None, None, None]


def draw_interior_inverse(key, part):
    table = symmetric_table(key, SUBDOMAIN_AXIAL * SUB_CI * NB, BLK, 1.0, 2.0, 0.6 / BLK ** 0.5)
    return table.reshape(SUBDOMAIN_AXIAL, SUB_CI, NB, BLK, BLK)


def draw_neumann_solve(key, part):
    table = symmetric_table(key, SUBDOMAIN_AXIAL * SUB_CI, B, 1.0, 2.0, 0.6 / B ** 0.5)
    return table.reshape(SUBDOMAIN_AXIAL, SUB_CI, B, B)


def draw_row_coarse(key, part):
    return symmetric_table(key, SUBDOMAIN_AXIAL, NP, 1.6, 2.8, 0.2)


def decay_table(key, slow_share):
    selection_key, baseline_key, noise_key, spike_key = jax.random.split(key, 4)
    slow = jax.random.uniform(selection_key, (NP,), jnp.float32) < slow_share
    slow_rate = jax.random.uniform(baseline_key, (NP,), jnp.float32, 0.01, 0.05)
    fast_rate = jax.random.uniform(jax.random.fold_in(baseline_key, 1), (NP,), jnp.float32, 0.35, 1.2)
    baseline_rate = jnp.where(slow, slow_rate, fast_rate)
    random_noise = jax.random.uniform(noise_key, (SUBDOMAIN_AXIAL, NP), jnp.float32, 0.7, 1.4)
    sudden_spike = jax.random.uniform(spike_key, (SUBDOMAIN_AXIAL, 1), jnp.float32) < 0.1
    return jnp.exp(-baseline_rate[None, :] * random_noise) * jnp.where(sudden_spike, 0.6, 1.0)


def draw_lower_coef(key, part):
    return decay_table(jax.random.fold_in(key, 5), 0.5)


def draw_upper_coef(key, part):
    return decay_table(jax.random.fold_in(key, 9), 0.5)


def face_permutations(key):
    keys = jax.random.split(key, SUBDOMAIN_AXIAL * SUB_CI * 4)
    perms = jax.vmap(lambda single: jax.random.permutation(single, F))(keys).astype(jnp.int32)
    offsets = jnp.arange(SUBDOMAIN_AXIAL * SUB_CI * 4, dtype=jnp.int32) % 4 * F
    return perms + offsets[:, None]


def draw_face_order(key, part):
    return face_permutations(jax.random.fold_in(key, 11)).reshape(SUBDOMAIN_AXIAL, SUB_CI, B).astype(jnp.int32)


def draw_primal_lists(key, part):
    perms = face_permutations(jax.random.fold_in(key, 13))
    return perms.reshape(SUBDOMAIN_AXIAL, SUB_CI, NP, LIST).astype(jnp.int32)


def shard_levels(rng, dims, pieces, least, high):
    def one(axis_at, shards_of):
        steps = jax.random.uniform(jax.random.fold_in(jax.random.fold_in(rng, 6), axis_at), (shards_of,), jnp.float32, least / len(pieces), high / len(pieces))
        return jnp.repeat(jnp.exp(steps), dims[axis_at] // shards_of).reshape((-1,) + (1,) * (len(dims) - axis_at - 1))

    loudness = one(*pieces[0])
    for cut in pieces[1:]:
        loudness = loudness * one(*cut)
    return loudness


def noise(own_key, dims, scale, most, shards=(), held_as=jnp.bfloat16):
    drawn = jax.random.normal(own_key, dims, jnp.float32) * scale
    if len(shards) > 0:
        drawn = shard_levels(own_key, dims, shards, -0.22, 0.18) * drawn
    return jnp.clip(drawn, min=-most, max=most).astype(held_as)


def setup_inputs(seed: int = 0) -> dict:
    seeds = jax.random.split(jax.random.key(seed), 12)
    return {
        "load_terms": draw_load_terms(jax.random.fold_in(seeds[11], 71), 0),
        "diffusivity": jnp.clip(jnp.exp(math.log(10.0) - 4.6051702 * jax.random.uniform(seeds[1], (SUBDOMAIN_AXIAL, SUB_CI, B), jnp.float32) ** shard_levels(seeds[1], (SUBDOMAIN_AXIAL, SUB_CI, B), ((0, 8), (1, 4)), -0.2, 0.2)), 0.1, 10.0),
        "interface_diag": jnp.clip(4.0 + 4.0 * jax.random.uniform(seeds[2], (SUBDOMAIN_AXIAL, SUB_CI, B), jnp.float32) ** shard_levels(seeds[2], (SUBDOMAIN_AXIAL, SUB_CI, B), ((0, 8), (1, 4)), -0.2, 0.2), 4.0, 8.0),
        "coupling": noise(seeds[3], (SUBDOMAIN_AXIAL, SUB_CI, B, NI), (4 * NI) ** -0.5, 0.125, ((0, 8), (1, 4)), jnp.float32),
        "interior_inverse": draw_interior_inverse(jax.random.fold_in(seeds[11], 71), 0),
        "neumann_solve": draw_neumann_solve(jax.random.fold_in(seeds[11], 71), 0),
        "row_coarse": draw_row_coarse(jax.random.fold_in(seeds[11], 71), 0),
        "lower_coef": draw_lower_coef(jax.random.fold_in(seeds[11], 71), 0),
        "upper_coef": draw_upper_coef(jax.random.fold_in(seeds[11], 71), 0),
        "face_order": draw_face_order(jax.random.fold_in(seeds[11], 71), 0),
        "primal_lists": draw_primal_lists(jax.random.fold_in(seeds[11], 71), 0),
    }


def invert_order(order):
    size = order.shape[0]
    return jnp.zeros((size,), jnp.int32).at[order].set(jnp.arange(size, dtype=jnp.int32))


def relabel(values, index):
    if values.ndim == 4:
        index = jnp.broadcast_to(index[:, :, None, :], values.shape)
    return jnp.take_along_axis(values, index, axis=-1)


def reference(load_terms, diffusivity, interface_diag, coupling, interior_inverse, neumann_solve, row_coarse, lower_coef, upper_coef, face_order, primal_lists):
    highest = lax.Precision.HIGHEST
    width = F
    flat_order = face_order.reshape(-1, B)
    inverse = jax.vmap(invert_order)(flat_order).reshape(face_order.shape)

    def assemble(values):
        shared = relabel(values, inverse)
        south = shared[..., :width]
        north = shared[..., width:2 * width]
        west = shared[..., 2 * width:3 * width]
        east = shared[..., 3 * width:]
        below = jnp.concatenate([jnp.zeros_like(north[:1]), north[:-1]], axis=0)
        above = jnp.concatenate([south[1:], jnp.zeros_like(south[:1])], axis=0)
        left_side = jnp.roll(east, 1, axis=1)
        right_side = jnp.roll(west, -1, axis=1)
        summed = jnp.concatenate([south + below, north + above, west + left_side, east + right_side], axis=-1)
        return relabel(summed, face_order)

    ends = jnp.ones((SUBDOMAIN_AXIAL, B), jnp.float32)
    ends = ends.at[0, :width].set(0.0).at[SUBDOMAIN_AXIAL - 1, width:2 * width].set(0.0)
    keep = ends[:, None, None, :]
    share = (diffusivity / assemble(diffusivity))[:, :, None, :]
    positions = jnp.arange(B, dtype=jnp.int32)
    averaging = jnp.sum((primal_lists[..., None] == positions).astype(jnp.float32), axis=3) / LIST

    def schur(direction):
        inner = jnp.einsum("acrb,acbi->acri", direction, coupling, precision=highest)
        blocked = inner.reshape(SUBDOMAIN_AXIAL, SUB_CI, R, NB, BLK)
        solved = jnp.einsum("acrnk,acnkl->acrnl", blocked, interior_inverse, precision=highest)
        solved = solved.reshape(SUBDOMAIN_AXIAL, SUB_CI, R, NI)
        back = jnp.einsum("acri,acbi->acrb", solved, coupling, precision=highest)
        return assemble(interface_diag[:, :, None, :] * direction - back) * keep

    def forward_step(carry, inputs):
        factor, value = inputs
        carry = factor * carry + (1.0 - factor) * value
        return carry, carry

    def precondition(residual):
        weighted = share * residual
        local_part = jnp.einsum("acrb,acbd->acrd", weighted, neumann_solve, precision=highest)
        primal = jnp.einsum("acrb,acpb->acrp", weighted, averaging, precision=highest)
        row_total = jnp.sum(primal, axis=1)
        row_part = jnp.einsum("arp,apq->arq", row_total, row_coarse, precision=highest)
        start = jnp.zeros((R, NP), jnp.float32)
        _, smoothed = lax.scan(forward_step, start, (lower_coef[:, None, :], row_total))
        _, top_part = lax.scan(forward_step, start, (upper_coef[:, None, :], smoothed), reverse=True)
        coarse = row_part + top_part
        coarse_part = jnp.einsum("arp,acpb->acrb", coarse, averaging, precision=highest)
        return assemble(share * (local_part + coarse_part)) * keep

    def inner_product(first, second):
        return 0.5 * jnp.sum(first * second, axis=(0, 1, 3))

    residual = assemble(load_terms) * keep
    solution_field = jnp.zeros_like(residual)
    precond = precondition(residual)
    direction = precond
    rz_value = inner_product(residual, precond)
    for iteration in range(ITERS):
        image = schur(direction)
        alpha = rz_value / inner_product(direction, image)
        solution_field = solution_field + alpha[None, None, :, None] * direction
        residual = residual - alpha[None, None, :, None] * image
        if iteration + 1 < ITERS:
            precond = precondition(residual)
            new_value = inner_product(residual, precond)
            direction = precond + (new_value / rz_value)[None, None, :, None] * direction
            rz_value = new_value
    return solution_field, residual
```

```python
import functools

import jax
import jax.numpy as jnp
from jax import lax
from jax.experimental import pallas as pl
from jax.experimental.pallas import tpu as pltpu
from jax.sharding import PartitionSpec as P

ITERS = 3
F32 = jnp.float32
BF16 = jnp.bfloat16
MESH = pl.DeviceIdType.MESH
NT = (((1,), (1,)), ((), ()))
HALOS = 1 + 2 * ITERS
SUMS = 2 * ITERS + 1


def split(value):
    high = value.astype(BF16)
    return high, (value - high.astype(F32)).astype(BF16)


def dot16(a, b, dims=(((1,), (0,)), ((), ()))):
    return lax.dot_general(a, b, dims, preferred_element_type=F32)


def kernel(
    rows,
    cols,
    load_ref,
    rho_ref,
    diag_ref,
    couple_ref,
    blocks_ref,
    neumann_ref,
    coarse_ref,
    lower_ref,
    upper_ref,
    order_ref,
    lists_ref,
    x_out,
    r_out,
    hout,
    hin,
    tile_out,
    tile_in,
    c_out,
    c_in,
    a_in,
    coef_in,
    perm,
    schur,
    neumann,
    half,
    vbuf,
    share,
    diag,
    mean,
    own_w,
    near_w,
    x,
    r,
    p,
    b,
    totals,
    hs,
    hr,
    ts,
    tr,
    cs,
    cr,
    as_,
    ar,
    fs,
    fr,
):
    k = lax.axis_index("axial")
    c = lax.axis_index("circ")
    width = perm.shape[1]
    block = blocks_ref.shape[-1]
    list_len = lists_ref.shape[-1]

    def circ_peer(d):
        return {"circ": lax.rem(c + d, cols)}

    def axial_peer(d):
        return {"axial": lax.rem(k + d, rows)}

    barrier = pltpu.get_barrier_semaphore()
    for d in range(1, cols):
        pl.semaphore_signal(barrier, inc=1, device_id=circ_peer(d), device_id_type=MESH)
    for d in range(1, rows):
        pl.semaphore_signal(barrier, inc=1, device_id=axial_peer(d), device_id_type=MESH)

    has = (k > 0, k < rows - 1)
    keep = [has[0].astype(F32), has[1].astype(F32)]

    def across(f):
        if f == 0:
            return {"axial": jnp.maximum(k - 1, 0)}
        if f == 1:
            return {"axial": jnp.minimum(k + 1, rows - 1)}
        return {"circ": lax.rem(c + (cols - 1 if f == 2 else 1), cols)}

    def face_copy(out, into, send, recv, t, f):
        return pltpu.make_async_remote_copy(
            src_ref=out.at[t, f],
            dst_ref=into.at[t, f ^ 1],
            send_sem=send.at[t, f],
            recv_sem=recv.at[t, f ^ 1],
            device_id=across(f),
            device_id_type=MESH,
        )

    def guarded(f, action):
        if f < 2:
            pl.when(has[f])(action)
        else:
            action()

    def send_face(args, t, f):
        guarded(f, lambda: face_copy(*args, t, f).start())

    def wait_face(args, t, f):
        guarded(f, lambda: face_copy(*args, t, f ^ 1).wait_recv())

    def done_face(args, t, f):
        guarded(f, lambda: face_copy(*args, t, f).wait_send())

    halo = (hout, hin, hs, hr)
    tiles = (tile_out, tile_in, ts, tr)

    for f in range(2):

        @pl.when(jnp.logical_not(has[f]))
        def _():
            tile_in[0, f] = jnp.zeros(tile_in.shape[2:], F32)
            for t in range(HALOS):
                hin[t, f] = jnp.zeros(hin.shape[2:], F32)

    sub = lax.broadcasted_iota(jnp.int32, (width, width), 0)
    lane = lax.broadcasted_iota(jnp.int32, (width, width), 1)
    list_sub = lax.broadcasted_iota(jnp.int32, (width, list_len), 0)

    def spread(column):
        return jnp.broadcast_to(column, (width, width))

    def pick(f):
        return perm[f].astype(F32)

    for f in range(4):
        span = pl.ds(f * width, width)
        one = (order_ref[0, :, span] - f * width == sub).astype(F32)
        perm[f] = one.astype(BF16)
        rho = jnp.sum(one * rho_ref[0, :, span], axis=1, keepdims=True)
        dia = jnp.sum(one * diag_ref[0, :, span], axis=1, keepdims=True)
        diag[f] = spread(dia)
        share[f] = spread(rho)
        member = []
        for i in range(2):
            named = (lists_ref[0, 0, pl.ds(2 * f + i, 1), :] - f * width == list_sub).astype(F32)
            member.append(jnp.sum(named, axis=1, keepdims=True))
        pair = jnp.where(lane == 0, member[0], jnp.where(lane == 1, member[1], 0.0))
        pair = dot16(one.astype(BF16), pair.astype(BF16)) / list_len
        mean[2 * f] = spread(pair[:, 0:1])
        mean[2 * f + 1] = spread(pair[:, 1:2])
        packed = jnp.where(
            lane == 0, rho, jnp.where(lane == 1, pair[:, 0:1], jnp.where(lane == 2, pair[:, 1:2], 0.0))
        )
        tile_out[0, f] = packed.T[0:8]
        hout[0, f] = lax.dot_general(
            one,
            load_ref[0, 0, :, span],
            NT,
            precision=lax.Precision.HIGHEST,
            preferred_element_type=F32,
        )

    pl.semaphore_wait(barrier, rows + cols - 2)
    for f in (2, 3, 0, 1):
        send_face(tiles, 0, f)
    for f in (2, 3, 0, 1):
        send_face(halo, 0, f)

    small_sub = lax.broadcasted_iota(jnp.int32, (8, 8), 0)
    small_lane = lax.broadcasted_iota(jnp.int32, (8, 8), 1)
    for i, ref in enumerate((lower_ref, upper_ref)):
        column = jnp.sum(jnp.where(small_sub == small_lane, ref[...], 0.0), axis=1, keepdims=True)
        coef_in[k, i] = jnp.broadcast_to(column, (8, width))

    def coef_copy(d):
        return pltpu.make_async_remote_copy(
            src_ref=coef_in.at[k],
            dst_ref=coef_in.at[k],
            send_sem=fs.at[d],
            recv_sem=fr.at[d],
            device_id=axial_peer(d),
            device_id_type=MESH,
        )

    def coef_arrival(d):
        row = lax.rem(k + rows - d, rows)
        return pltpu.make_async_remote_copy(
            src_ref=coef_in.at[row],
            dst_ref=coef_in.at[row],
            send_sem=fs.at[d],
            recv_sem=fr.at[d],
            device_id=axial_peer(d),
            device_id_type=MESH,
        )

    for d in range(1, rows):
        coef_copy(d).start()

    for f in (0, 1, 2, 3):
        wait_face(tiles, 0, f)
        got = jnp.concatenate([tile_in[0, f], jnp.zeros((width - 8, width), F32)], axis=0).T
        mine = share[f]
        theirs = spread(got[:, 0:1])
        both = mine + theirs
        own_share = mine / both
        near_share = theirs / both
        share[f] = own_share
        masked = own_share * keep[f] if f < 2 else own_share
        for i in range(2):
            own_w[2 * f + i] = masked * mean[2 * f + i]
            near_w[2 * f + i] = near_share * spread(got[:, 1 + i : 2 + i])

    def circ_copy(t, n, d):
        return pltpu.make_async_remote_copy(
            src_ref=c_out.at[t, pl.ds(0, n)],
            dst_ref=c_in.at[t, d, pl.ds(0, n)],
            send_sem=cs.at[t, d],
            recv_sem=cr.at[t, d],
            device_id=circ_peer(d),
            device_id_type=MESH,
        )

    def axial_copy(t, n, d, row):
        return pltpu.make_async_remote_copy(
            src_ref=a_in.at[t, row, pl.ds(0, n)],
            dst_ref=a_in.at[t, row, pl.ds(0, n)],
            send_sem=as_.at[t, d],
            recv_sem=ar.at[t, d],
            device_id=axial_peer(d),
            device_id_type=MESH,
        )

    sizes = {}

    def sum_begin(t, n, value):
        sizes[t] = n
        c_out[t, pl.ds(0, n)] = value
        for d in range(1, cols):
            circ_copy(t, n, d).start()

    def sum_middle(t):
        n = sizes[t]
        value = c_out[t, pl.ds(0, n)]
        for d in range(1, cols):
            circ_copy(t, n, d).wait_recv()
            value = value + c_in[t, d, pl.ds(0, n)]
        a_in[t, k, pl.ds(0, n)] = value
        for d in range(1, rows):
            axial_copy(t, n, d, k).start()

    def sum_end(t):
        n = sizes[t]
        for d in range(1, rows):
            axial_copy(t, n, d, lax.rem(k + rows - d, rows)).wait_recv()

    def dot_total(t, start):
        value = a_in[t, 0, pl.ds(start, 1)]
        for m in range(1, rows):
            value = value + a_in[t, m, pl.ds(start, 1)]
        return 0.0 + value

    sub8 = lax.broadcasted_iota(jnp.int32, (8, width), 0)

    def constraint_tiles(field, extra):
        def one(table, index, f):
            return jnp.sum(table[index] * field(f), axis=0, keepdims=True)

        first = []
        for q in range(8):
            value = own_w[q] * field(q // 2)
            if q in (4, 5):
                value = value + near_w[q + 2] * field(3)
            if q in (6, 7):
                value = value + near_w[q - 2] * field(2)
            first.append(jnp.sum(value, axis=0, keepdims=True))
        second = [one(near_w, 2, 1), one(near_w, 3, 1), one(near_w, 0, 0), one(near_w, 1, 0)]
        second = second + [extra] + [jnp.zeros((1, width), F32)] * 3
        return jnp.concatenate(first + second, axis=0)

    def row_totals(t, m):
        value = a_in[t, m, pl.ds(0, 8)]
        if m > 0:
            value = value + jnp.where(sub8 < 2, a_in[t, m - 1, pl.ds(8, 8)], 0.0)
        if m < rows - 1:
            value = value + jnp.where(
                jnp.logical_and(sub8 >= 2, sub8 < 4), a_in[t, m + 1, pl.ds(8, 8)], 0.0
            )
        return value

    sum_begin(0, 16, constraint_tiles(lambda f: hout[0, f], jnp.zeros((1, width), F32)))

    def store_pair(table, f, cut, value):
        high, low = split(value)
        table[f, pl.ds(0, width), cut] = high
        table[f, pl.ds(width, width), cut] = low

    for f in range(4):
        rows_f = pl.ds(f * width, width)
        high, low = split(neumann_ref[0, 0, rows_f, :])
        high = dot16(perm[f], high).astype(BF16)
        low = dot16(perm[f], low).astype(BF16)
        for g in range(4):
            cut = slice(g * width, (g + 1) * width)
            span = pl.ds(g * width, width)
            neumann[f, pl.ds(0, width), span] = dot16(high[:, cut], perm[g], NT).astype(BF16)
            neumann[f, pl.ds(width, width), span] = dot16(low[:, cut], perm[g], NT).astype(BF16)

    sum_middle(0)

    def apply(table, field):
        for f in range(4):
            high, low = split(field(f))
            vbuf[pl.ds(f * width, width), pl.ds(0, width)] = high
            vbuf[pl.ds(f * width, width), pl.ds(width, width)] = low

        def one(f):
            full = dot16(table[f], vbuf[...])
            small = full[:width, width:] + full[width:, :width] + full[width:, width:]
            return full[:width, :width] + small

        return one

    def assembled(t, f):
        value = hout[t, f] + hin[t, f]
        return value * keep[f] if f < 2 else value

    def coarse_value():
        smooth = []
        h = jnp.zeros((8, width), F32)
        for m in range(rows):
            factor = coef_in[m, 0]
            h = factor * h + (1.0 - factor) * totals[m]
            smooth.append(h)
        top = jnp.zeros((8, width), F32)
        mine = jnp.zeros((8, width), F32)
        for m in reversed(range(rows)):
            factor = coef_in[m, 1]
            top = factor * top + (1.0 - factor) * smooth[m]
            mine = mine + jnp.where(k == m, top, 0.0)
        own = totals[k]
        for q in range(8):
            mine = mine + coarse_ref[0, :, pl.ds(q, 1)] * own[q : q + 1]
        return mine

    def precondition(t, s):
        local = apply(neumann, lambda f: share[f] * r[f])
        coarse = coarse_value()
        partial = None
        for f in (2, 3, 0, 1):
            value = local(f)
            for i in range(2):
                q = 2 * f + i
                value = value + mean[q] * coarse[q : q + 1]
            value = share[f] * value
            hout[t, f] = value
            send_face(halo, t, f)
            term = jnp.sum(r[f] * value, axis=0, keepdims=True)
            partial = term if partial is None else partial + term
        sum_begin(s, 8, jnp.broadcast_to(partial, (8, width)))

    for f in (0, 1, 2, 3):
        wait_face(halo, 0, f)
        r[f] = assembled(0, f)
    sum_end(0)
    for d in range(1, rows):
        coef_arrival(d).wait_recv()
    for m in range(rows):
        totals[m] = row_totals(0, m)
    precondition(1, 1)

    for f in range(4):
        span = pl.ds(f * width, width)
        high, low = split(couple_ref[0, 0, span, :])
        half[0, span, :] = dot16(perm[f], high).astype(BF16)
        half[1, span, :] = dot16(perm[f], low).astype(BF16)
    sum_middle(1)
    for n in range(blocks_ref.shape[2]):
        cut = pl.ds(n * block, block)
        ih, il = split(blocks_ref[0, 0, n])
        ch, cl = half[0, :, cut], half[1, :, cut]
        high, low = split(dot16(ch, ih) + (dot16(ch, il) + dot16(cl, ih)))
        half[2, :, cut] = high
        half[3, :, cut] = low
    for f in range(4):
        span = pl.ds(f * width, width)
        eh, el = half[2, span, :], half[3, span, :]
        ch, cl = half[0], half[1]
        value = dot16(eh, ch, NT) + (dot16(eh, cl, NT) + dot16(el, ch, NT))
        store_pair(schur, f, slice(None), value)

    rz = None
    for step in range(ITERS):
        t = 1 + 2 * step
        for f in (0, 1, 2, 3):
            wait_face(halo, t, f)
        back = apply(schur, lambda f: assembled(t, f))
        if step > 0:
            sum_middle(t)
            sum_end(t)
            new = dot_total(t, 0)
            beta = new / rz
        else:
            sum_end(t)
            new = dot_total(t, 0)
            beta = None
        rz = new
        partial = None
        for f in (2, 3, 0, 1):
            z = assembled(t, f)
            value = diag[f] * z - back(f)
            if beta is not None:
                value = value + beta * hout[t - 1, f]
                z = z + beta * p[f]
            p[f] = z
            hout[t + 1, f] = value
            send_face(halo, t + 1, f)
            term = jnp.sum(z * value, axis=0, keepdims=True)
            partial = term if partial is None else partial + term
        last = step + 1 == ITERS
        if last:
            sum_begin(t + 1, 8, jnp.broadcast_to(partial, (8, width)))
        else:
            sum_begin(t + 1, 16, constraint_tiles(lambda f: hout[t + 1, f], partial))
        sum_middle(t + 1)
        for f in (0, 1, 2, 3):
            wait_face(halo, t + 1, f)
        sum_end(t + 1)
        alpha = rz / dot_total(t + 1, 0 if last else 12)
        for f in range(4):
            x[f] = alpha * p[f] if step == 0 else x[f] + alpha * p[f]
            r[f] = r[f] - alpha * assembled(t + 1, f)
        if not last:
            for m in range(rows):
                totals[m] = totals[m] - alpha * row_totals(t + 1, m)
            precondition(t + 2, t + 2)

    for f in range(4):
        span = pl.ds(f * width, width)
        one = pick(f)
        for ref, field in ((x_out, x), (r_out, r)):
            ref[0, 0, :, span] = jnp.dot(
                field[f].T, one, precision=lax.Precision.HIGHEST, preferred_element_type=F32
            )

    for f in range(4):
        done_face(tiles, 0, f)
        for t in range(HALOS):
            done_face(halo, t, f)
    for d in range(1, rows):
        coef_copy(d).wait_send()
    for t in range(SUMS):
        for d in range(1, cols):
            circ_copy(t, sizes[t], d).wait_send()
        for d in range(1, rows):
            axial_copy(t, sizes[t], d, k).wait_send()


def local(rows, cols, *args):
    load = args[0]
    count, points = load.shape[2:]
    width = points // 4
    dma = pltpu.SemaphoreType.DMA
    face = (4, width, width)
    scratch = [
        pltpu.VMEM((HALOS,) + face, F32),
        pltpu.VMEM((HALOS,) + face, F32),
        pltpu.VMEM((1, 4, 8, width), F32),
        pltpu.VMEM((1, 4, 8, width), F32),
        pltpu.VMEM((SUMS, 16, width), F32),
        pltpu.VMEM((SUMS, cols, 16, width), F32),
        pltpu.VMEM((SUMS, rows, 16, width), F32),
        pltpu.VMEM((rows, 2, 8, width), F32),
        pltpu.VMEM(face, BF16),
        pltpu.VMEM((4, 2 * width, points), BF16),
        pltpu.VMEM((4, 2 * width, points), BF16),
        pltpu.VMEM((4, points, args[3].shape[-1]), BF16),
        pltpu.VMEM((points, 2 * width), BF16),
        pltpu.VMEM(face, F32),
        pltpu.VMEM(face, F32),
        pltpu.VMEM((8, width, width), F32),
        pltpu.VMEM((8, width, width), F32),
        pltpu.VMEM((8, width, width), F32),
        pltpu.VMEM(face, F32),
        pltpu.VMEM(face, F32),
        pltpu.VMEM(face, F32),
        pltpu.VMEM(face, F32),
        pltpu.VMEM((rows, 8, width), F32),
        dma((HALOS, 4)),
        dma((HALOS, 4)),
        dma((1, 4)),
        dma((1, 4)),
        dma((SUMS, cols)),
        dma((SUMS, cols)),
        dma((SUMS, rows)),
        dma((SUMS, rows)),
        dma((rows,)),
        dma((rows,)),
    ]
    shape = jax.ShapeDtypeStruct(load.shape, F32)
    return pl.pallas_call(
        functools.partial(kernel, rows, cols),
        out_shape=(shape, shape),
        in_specs=[pl.BlockSpec(memory_space=pltpu.VMEM)] * len(args),
        out_specs=(pl.BlockSpec(memory_space=pltpu.VMEM),) * 2,
        scratch_shapes=scratch,
        compiler_params=pltpu.CompilerParams(
            collective_id=0, has_side_effects=True, vmem_limit_bytes=40 * 2**20
        ),
    )(*args)


def solution(mesh):
    in_specs = (
        P("axial", "circ", None, None),
        P("axial", "circ", None),
        P("axial", "circ", None),
        P("axial", "circ", None, None),
        P("axial", "circ", None, None, None),
        P("axial", "circ", None, None),
        P("axial", None, None),
        P("axial", None),
        P("axial", None),
        P("axial", "circ", None),
        P("axial", "circ", None, None),
    )
    out_specs = (P("axial", "circ", None, None), P("axial", "circ", None, None))
    body = functools.partial(local, mesh.shape["axial"], mesh.shape["circ"])
    return jax.shard_map(body, mesh=mesh, in_specs=in_specs, out_specs=out_specs, check_vma=False)
```

```python
import functools

import jax
import jax.numpy as jnp
from jax import lax
from jax.experimental import pallas as pl
from jax.experimental.pallas import tpu as pltpu
from jax.sharding import PartitionSpec as P

ITERS = 3
F32 = jnp.float32
BF16 = jnp.bfloat16
MESH = pl.DeviceIdType.MESH
NT = (((1,), (1,)), ((), ()))
HALOS = 1 + 2 * ITERS
SUMS = 1 + ITERS


def split(value):
    high = value.astype(BF16)
    return high, (value - high.astype(F32)).astype(BF16)


def dot16(a, b, dims=(((1,), (0,)), ((), ()))):
    return lax.dot_general(a, b, dims, preferred_element_type=F32)


def kernel(
    rows,
    cols,
    *refs,
):
    sources, refs = refs[:11], refs[11:]
    (x_out, r_out), refs = refs[:2], refs[2:]
    held, in_sem, refs = refs[:11], refs[11], refs[12:]
    (
        load_ref, rho_ref, diag_ref, couple_ref, blocks_ref, neumann_ref,
        coarse_ref, lower_ref, upper_ref, order_ref, lists_ref,
    ) = held
    (
        hout, hin, tile_out, tile_in, c_out, c_in, a_in, coef_in, perm, schur, neumann, half, vbuf,
        share, diag, mean, own_w, near_w, x, r, p, image, totals, moved,
        hs, hr, ts, tr, cs, cr, as_, ar, fs, fr,
    ) = refs
    k = lax.axis_index("axial")
    c = lax.axis_index("circ")
    width = perm.shape[1]
    arrivals = [
        pltpu.make_async_copy(source, target, in_sem.at[i])
        for i, (source, target) in enumerate(zip(sources, held))
    ]
    for i in (9, 1, 2, 10, 0, 7, 8, 6, 5, 3, 4):
        arrivals[i].start()
    block = blocks_ref.shape[-1]
    list_len = lists_ref.shape[-1]

    def circ_peer(d):
        return {"circ": lax.rem(c + d, cols)}

    def axial_peer(d):
        return {"axial": lax.rem(k + d, rows)}

    barrier = pltpu.get_barrier_semaphore()
    for d in range(1, cols):
        pl.semaphore_signal(barrier, inc=1, device_id=circ_peer(d), device_id_type=MESH)
    for d in range(1, rows):
        pl.semaphore_signal(barrier, inc=1, device_id=axial_peer(d), device_id_type=MESH)

    has = (k > 0, k < rows - 1)
    keep = [has[0].astype(F32), has[1].astype(F32)]

    def across(f):
        if f == 0:
            return {"axial": jnp.maximum(k - 1, 0)}
        if f == 1:
            return {"axial": jnp.minimum(k + 1, rows - 1)}
        return {"circ": lax.rem(c + (cols - 1 if f == 2 else 1), cols)}

    def face_copy(out, into, send, recv, t, f):
        return pltpu.make_async_remote_copy(
            src_ref=out.at[t, f],
            dst_ref=into.at[t, f ^ 1],
            send_sem=send.at[t, f],
            recv_sem=recv.at[t, f ^ 1],
            device_id=across(f),
            device_id_type=MESH,
        )

    def guarded(f, action):
        if f < 2:
            pl.when(has[f])(action)
        else:
            action()

    def send_face(args, t, f):
        guarded(f, lambda: face_copy(*args, t, f).start())

    def wait_face(args, t, f):
        guarded(f, lambda: face_copy(*args, t, f ^ 1).wait_recv())

    def done_face(args, t, f):
        guarded(f, lambda: face_copy(*args, t, f).wait_send())

    halo = (hout, hin, hs, hr)
    tiles = (tile_out, tile_in, ts, tr)

    for f in range(2):

        @pl.when(jnp.logical_not(has[f]))
        def _():
            tile_in[0, f] = jnp.zeros(tile_in.shape[2:], F32)
            for t in range(HALOS):
                hin[t, f] = jnp.zeros(hin.shape[2:], F32)

    sub = lax.broadcasted_iota(jnp.int32, (width, width), 0)
    lane = lax.broadcasted_iota(jnp.int32, (width, width), 1)
    list_sub = lax.broadcasted_iota(jnp.int32, (width, list_len), 0)

    def spread(column):
        return jnp.broadcast_to(column, (width, width))

    def pick(f):
        return perm[f].astype(F32)

    for i in (9, 1, 2, 10, 0):
        arrivals[i].wait()

    for f in range(4):
        span = pl.ds(f * width, width)
        one = (order_ref[0, :, span] - f * width == sub).astype(F32)
        perm[f] = one.astype(BF16)
        rho = jnp.sum(one * rho_ref[0, :, span], axis=1, keepdims=True)
        dia = jnp.sum(one * diag_ref[0, :, span], axis=1, keepdims=True)
        diag[f] = spread(dia)
        share[f] = spread(rho)
        member = []
        for i in range(2):
            named = (lists_ref[0, 0, pl.ds(2 * f + i, 1), :] - f * width == list_sub).astype(F32)
            member.append(jnp.sum(named, axis=1, keepdims=True))
        pair = jnp.where(lane == 0, member[0], jnp.where(lane == 1, member[1], 0.0))
        pair = dot16(one.astype(BF16), pair.astype(BF16)) / list_len
        mean[2 * f] = spread(pair[:, 0:1])
        mean[2 * f + 1] = spread(pair[:, 1:2])
        packed = jnp.where(
            lane == 0, rho, jnp.where(lane == 1, pair[:, 0:1], jnp.where(lane == 2, pair[:, 1:2], 0.0))
        )
        tile_out[0, f] = packed.T[0:8]
        hout[0, f] = lax.dot_general(
            one,
            load_ref[0, 0, :, span],
            NT,
            precision=lax.Precision.HIGHEST,
            preferred_element_type=F32,
        )

    pl.semaphore_wait(barrier, rows + cols - 2)
    for f in (2, 3, 0, 1):
        send_face(tiles, 0, f)
    for f in (2, 3, 0, 1):
        send_face(halo, 0, f)

    for i in (7, 8, 6):
        arrivals[i].wait()

    small_sub = lax.broadcasted_iota(jnp.int32, (8, 8), 0)
    small_lane = lax.broadcasted_iota(jnp.int32, (8, 8), 1)
    for i, ref in enumerate((lower_ref, upper_ref)):
        column = jnp.sum(jnp.where(small_sub == small_lane, ref[...], 0.0), axis=1, keepdims=True)
        coef_in[k, i] = jnp.broadcast_to(column, (8, width))

    def coef_copy(d):
        return pltpu.make_async_remote_copy(
            src_ref=coef_in.at[k],
            dst_ref=coef_in.at[k],
            send_sem=fs.at[d],
            recv_sem=fr.at[d],
            device_id=axial_peer(d),
            device_id_type=MESH,
        )

    def coef_arrival(d):
        row = lax.rem(k + rows - d, rows)
        return pltpu.make_async_remote_copy(
            src_ref=coef_in.at[row],
            dst_ref=coef_in.at[row],
            send_sem=fs.at[d],
            recv_sem=fr.at[d],
            device_id=axial_peer(d),
            device_id_type=MESH,
        )

    for d in range(1, rows):
        coef_copy(d).start()

    for f in (0, 1, 2, 3):
        wait_face(tiles, 0, f)
        got = jnp.concatenate([tile_in[0, f], jnp.zeros((width - 8, width), F32)], axis=0).T
        mine = share[f]
        theirs = spread(got[:, 0:1])
        both = mine + theirs
        own_share = mine / both
        near_share = theirs / both
        share[f] = own_share
        masked = own_share * keep[f] if f < 2 else own_share
        for i in range(2):
            own_w[2 * f + i] = masked * mean[2 * f + i]
            near_w[2 * f + i] = near_share * spread(got[:, 1 + i : 2 + i])

    def span_of(t):
        return pl.ds(8, 8) if t == ITERS else pl.ds(0, 16)

    def circ_copy(t, d):
        return pltpu.make_async_remote_copy(
            src_ref=c_out.at[t, span_of(t)],
            dst_ref=c_in.at[t, d, span_of(t)],
            send_sem=cs.at[t, d],
            recv_sem=cr.at[t, d],
            device_id=circ_peer(d),
            device_id_type=MESH,
        )

    def axial_copy(t, d, row):
        return pltpu.make_async_remote_copy(
            src_ref=a_in.at[t, row, span_of(t)],
            dst_ref=a_in.at[t, row, span_of(t)],
            send_sem=as_.at[t, d],
            recv_sem=ar.at[t, d],
            device_id=axial_peer(d),
            device_id_type=MESH,
        )

    def sum_begin(t, value):
        c_out[t, span_of(t)] = value
        for d in range(1, cols):
            circ_copy(t, d).start()

    def sum_middle(t):
        value = c_out[t, span_of(t)]
        for d in range(1, cols):
            circ_copy(t, d).wait_recv()
            value = value + c_in[t, d, span_of(t)]
        a_in[t, k, span_of(t)] = value
        for d in range(1, rows):
            axial_copy(t, d, k).start()

    def sum_end(t):
        for d in range(1, rows):
            axial_copy(t, d, lax.rem(k + rows - d, rows)).wait_recv()

    def dot_total(t, row):
        value = a_in[t, 0, pl.ds(row, 1)]
        for m in range(1, rows):
            value = value + a_in[t, m, pl.ds(row, 1)]
        return value

    sub8 = lax.broadcasted_iota(jnp.int32, (8, width), 0)

    def dot_tile(dots, head):
        dots = dots + [jnp.zeros((1, width), F32)] * (4 - len(dots))
        return jnp.concatenate(head + dots, axis=0)

    def constraint_tiles(field, dots):
        def one(table, index, f):
            return jnp.sum(table[index] * field(f), axis=0, keepdims=True)

        first = []
        for q in range(8):
            value = own_w[q] * field(q // 2)
            if q in (4, 5):
                value = value + near_w[q + 2] * field(3)
            if q in (6, 7):
                value = value + near_w[q - 2] * field(2)
            first.append(jnp.sum(value, axis=0, keepdims=True))
        second = [one(near_w, 2, 1), one(near_w, 3, 1), one(near_w, 0, 0), one(near_w, 1, 0)]
        return dot_tile(dots, first + second)

    def row_totals(t, m):
        value = a_in[t, m, pl.ds(0, 8)]
        if m > 0:
            value = value + jnp.where(sub8 < 2, a_in[t, m - 1, pl.ds(8, 8)], 0.0)
        if m < rows - 1:
            value = value + jnp.where(
                jnp.logical_and(sub8 >= 2, sub8 < 4), a_in[t, m + 1, pl.ds(8, 8)], 0.0
            )
        return value

    sum_begin(0, constraint_tiles(lambda f: hout[0, f], []))

    arrivals[5].wait()

    def store_pair(table, f, cut, value):
        high, low = split(value)
        table[f, pl.ds(0, width), cut] = high
        table[f, pl.ds(width, width), cut] = low

    for f in range(4):
        rows_f = pl.ds(f * width, width)
        high, low = split(neumann_ref[0, 0, rows_f, :])
        high = dot16(perm[f], high).astype(BF16)
        low = dot16(perm[f], low).astype(BF16)
        for g in range(4):
            cut = slice(g * width, (g + 1) * width)
            span = pl.ds(g * width, width)
            neumann[f, pl.ds(0, width), span] = dot16(high[:, cut], perm[g], NT).astype(BF16)
            neumann[f, pl.ds(width, width), span] = dot16(low[:, cut], perm[g], NT).astype(BF16)

    sum_middle(0)

    def apply(table, field):
        for f in range(4):
            high, low = split(field(f))
            vbuf[pl.ds(f * width, width), pl.ds(0, width)] = high
            vbuf[pl.ds(f * width, width), pl.ds(width, width)] = low

        def one(f):
            full = dot16(table[f], vbuf[...])
            small = full[:width, width:] + full[width:, :width] + full[width:, width:]
            return full[:width, :width] + small

        return one

    def assembled(t, f):
        value = hout[t, f] + hin[t, f]
        return value * keep[f] if f < 2 else value

    def coarse_value():
        smooth = []
        h = jnp.zeros((8, width), F32)
        for m in range(rows):
            factor = coef_in[m, 0]
            h = factor * h + (1.0 - factor) * totals[m]
            smooth.append(h)
        top = jnp.zeros((8, width), F32)
        mine = jnp.zeros((8, width), F32)
        for m in reversed(range(rows)):
            factor = coef_in[m, 1]
            top = factor * top + (1.0 - factor) * smooth[m]
            mine = mine + jnp.where(k == m, top, 0.0)
        own = totals[k]
        for q in range(8):
            mine = mine + coarse_ref[0, :, pl.ds(q, 1)] * own[q : q + 1]
        return mine

    def precondition(t):
        local = apply(neumann, lambda f: share[f] * r[f])
        coarse = coarse_value()
        for f in (2, 3, 0, 1):
            value = local(f)
            for i in range(2):
                q = 2 * f + i
                value = value + mean[q] * coarse[q : q + 1]
            value = share[f] * value
            hout[t, f] = value
            send_face(halo, t, f)

    for f in (0, 1, 2, 3):
        wait_face(halo, 0, f)
        r[f] = assembled(0, f)
    sum_end(0)
    for d in range(1, rows):
        coef_arrival(d).wait_recv()
    for m in range(rows):
        totals[m] = row_totals(0, m)
    precondition(1)

    arrivals[3].wait()
    arrivals[4].wait()

    for f in range(4):
        span = pl.ds(f * width, width)
        high, low = split(couple_ref[0, 0, span, :])
        half[0, span, :] = dot16(perm[f], high).astype(BF16)
        half[1, span, :] = dot16(perm[f], low).astype(BF16)
    for n in range(blocks_ref.shape[2]):
        cut = pl.ds(n * block, block)
        ih, il = split(blocks_ref[0, 0, n])
        ch, cl = half[0, :, cut], half[1, :, cut]
        high, low = split(dot16(ch, ih) + (dot16(ch, il) + dot16(cl, ih)))
        half[2, :, cut] = high
        half[3, :, cut] = low
    for f in range(4):
        span = pl.ds(f * width, width)
        eh, el = half[2, span, :], half[3, span, :]
        ch, cl = half[0], half[1]
        value = dot16(eh, ch, NT) + (dot16(eh, cl, NT) + dot16(el, ch, NT))
        store_pair(schur, f, slice(None), value)

    def fold(value):
        return jnp.sum(value, axis=0, keepdims=True)

    rz = None
    pap = None
    for step in range(ITERS):
        t = 1 + 2 * step
        last = step + 1 == ITERS
        for f in (0, 1, 2, 3):
            wait_face(halo, t, f)
        back = apply(schur, lambda f: assembled(t, f))
        dots = [jnp.zeros((1, width), F32) for _ in range(2 if step == 0 else 3)]
        for f in (2, 3, 0, 1):
            z = assembled(t, f)
            value = diag[f] * z - back(f)
            hout[t + 1, f] = value
            dots[0] = dots[0] + 0.5 * fold(r[f] * z)
            dots[1] = dots[1] + fold(z * value)
            if step > 0:
                dots[2] = dots[2] + fold(0.5 * (z * image[f]) + p[f] * value)
        if last:
            sum_begin(step + 1, dot_tile(dots, [jnp.zeros((1, width), F32)] * 4))
        else:
            sum_begin(step + 1, constraint_tiles(lambda f: hout[t + 1, f], dots))
        for f in (2, 3, 0, 1):
            send_face(halo, t + 1, f)
        sum_middle(step + 1)
        for f in (0, 1, 2, 3):
            wait_face(halo, t + 1, f)
        sum_end(step + 1)
        new = dot_total(step + 1, 12)
        new_pap = dot_total(step + 1, 13)
        if step > 0:
            beta = new / rz
            new_pap = new_pap + beta * (dot_total(step + 1, 14) + beta * pap)
        rz, pap = new, new_pap
        alpha = rz / pap
        for f in range(4):
            z = assembled(t, f)
            w = assembled(t + 1, f)
            if step > 0:
                z = z + beta * p[f]
                w = w + beta * image[f]
            p[f] = z
            image[f] = w
            x[f] = alpha * z if step == 0 else x[f] + alpha * z
            r[f] = r[f] - alpha * w
        if not last:
            for m in range(rows):
                value = row_totals(step + 1, m)
                if step > 0:
                    value = value + beta * moved[m]
                moved[m] = value
                totals[m] = totals[m] - alpha * value
            precondition(t + 2)

    for f in range(4):
        span = pl.ds(f * width, width)
        one = pick(f)
        for ref, field in ((x_out, x), (r_out, r)):
            ref[0, 0, :, span] = jnp.dot(
                field[f].T, one, precision=lax.Precision.HIGHEST, preferred_element_type=F32
            )

    for f in range(4):
        done_face(tiles, 0, f)
        for t in range(HALOS):
            done_face(halo, t, f)
    for d in range(1, rows):
        coef_copy(d).wait_send()
    for t in range(SUMS):
        for d in range(1, cols):
            circ_copy(t, d).wait_send()
        for d in range(1, rows):
            axial_copy(t, d, k).wait_send()


def local(rows, cols, *args):
    load = args[0]
    count, points = load.shape[2:]
    width = points // 4
    dma = pltpu.SemaphoreType.DMA
    face = (4, width, width)
    scratch = [pltpu.VMEM(arg.shape, arg.dtype) for arg in args] + [
        dma((len(args),)),
        pltpu.VMEM((HALOS,) + face, F32),
        pltpu.VMEM((HALOS,) + face, F32),
        pltpu.VMEM((1, 4, 8, width), F32),
        pltpu.VMEM((1, 4, 8, width), F32),
        pltpu.VMEM((SUMS, 16, width), F32),
        pltpu.VMEM((SUMS, cols, 16, width), F32),
        pltpu.VMEM((SUMS, rows, 16, width), F32),
        pltpu.VMEM((rows, 2, 8, width), F32),
        pltpu.VMEM(face, BF16),
        pltpu.VMEM((4, 2 * width, points), BF16),
        pltpu.VMEM((4, 2 * width, points), BF16),
        pltpu.VMEM((4, points, args[3].shape[-1]), BF16),
        pltpu.VMEM((points, 2 * width), BF16),
        pltpu.VMEM(face, F32),
        pltpu.VMEM(face, F32),
        pltpu.VMEM((8, width, width), F32),
        pltpu.VMEM((8, width, width), F32),
        pltpu.VMEM((8, width, width), F32),
        pltpu.VMEM(face, F32),
        pltpu.VMEM(face, F32),
        pltpu.VMEM(face, F32),
        pltpu.VMEM(face, F32),
        pltpu.VMEM((rows, 8, width), F32),
        pltpu.VMEM((rows, 8, width), F32),
        dma((HALOS, 4)),
        dma((HALOS, 4)),
        dma((1, 4)),
        dma((1, 4)),
        dma((SUMS, cols)),
        dma((SUMS, cols)),
        dma((SUMS, rows)),
        dma((SUMS, rows)),
        dma((rows,)),
        dma((rows,)),
    ]
    shape = jax.ShapeDtypeStruct(load.shape, F32)
    return pl.pallas_call(
        functools.partial(kernel, rows, cols),
        out_shape=(shape, shape),
        in_specs=[pl.BlockSpec(memory_space=pl.ANY)] * len(args),
        out_specs=(pl.BlockSpec(memory_space=pltpu.VMEM),) * 2,
        scratch_shapes=scratch,
        compiler_params=pltpu.CompilerParams(
            collective_id=0, has_side_effects=True, vmem_limit_bytes=56 * 2**20
        ),
    )(*args)


def solution(mesh):
    in_specs = (
        P("axial", "circ", None, None),
        P("axial", "circ", None),
        P("axial", "circ", None),
        P("axial", "circ", None, None),
        P("axial", "circ", None, None, None),
        P("axial", "circ", None, None),
        P("axial", None, None),
        P("axial", None),
        P("axial", None),
        P("axial", "circ", None),
        P("axial", "circ", None, None),
    )
    out_specs = (P("axial", "circ", None, None), P("axial", "circ", None, None))
    body = functools.partial(local, mesh.shape["axial"], mesh.shape["circ"])
    return jax.shard_map(body, mesh=mesh, in_specs=in_specs, out_specs=out_specs, check_vma=False)
```

```python
import functools

import jax
import jax.numpy as jnp
from jax import lax
from jax.experimental import pallas as pl
from jax.experimental.pallas import tpu as pltpu
from jax.sharding import PartitionSpec as P

ITERS = 3
F32 = jnp.float32
BF16 = jnp.bfloat16
MESH = pl.DeviceIdType.MESH
NT = (((1,), (1,)), ((), ()))
HALOS = 1 + 2 * ITERS
SUMS = 1 + ITERS
GROUPS = 2


def split(value):
    high = value.astype(BF16)
    return high, (value - high.astype(F32)).astype(BF16)


def dot16(a, b, dims=(((1,), (0,)), ((), ()))):
    return lax.dot_general(a, b, dims, preferred_element_type=F32)


def kernel(
    rows,
    cols,
    *refs,
):
    sources, refs = refs[:11], refs[11:]
    (x_out, r_out), refs = refs[:2], refs[2:]
    held, in_sem, refs = refs[:11], refs[11], refs[12:]
    (
        load_ref, rho_ref, diag_ref, couple_ref, blocks_ref, neumann_ref,
        coarse_ref, lower_ref, upper_ref, order_ref, lists_ref,
    ) = held
    (
        hout, hin, tile_out, tile_in, c_out, c_in, a_in, coef_in, perm, schur, neumann, half, vbuf,
        share, diag, mean, own_w, near_w, x, r, p, image, totals, moved,
        hs, hr, ts, tr, cs, cr, as_, ar, fs, fr,
    ) = refs
    k = lax.axis_index("axial")
    c = lax.axis_index("circ")
    width = perm.shape[1]
    fold_rows = width // GROUPS
    arrivals = [
        pltpu.make_async_copy(source, target, in_sem.at[i])
        for i, (source, target) in enumerate(zip(sources, held))
    ]
    for i in (9, 1, 2, 10, 0, 7, 8, 6, 5, 3, 4):
        arrivals[i].start()
    block = blocks_ref.shape[-1]
    list_len = lists_ref.shape[-1]

    def circ_peer(d):
        return {"circ": lax.rem(c + d, cols)}

    def axial_peer(d):
        return {"axial": lax.rem(k + d, rows)}

    barrier = pltpu.get_barrier_semaphore()
    for d in range(1, cols):
        pl.semaphore_signal(barrier, inc=1, device_id=circ_peer(d), device_id_type=MESH)
    for d in range(1, rows):
        pl.semaphore_signal(barrier, inc=1, device_id=axial_peer(d), device_id_type=MESH)

    has = (k > 0, k < rows - 1)
    keep = [has[0].astype(F32), has[1].astype(F32)]

    def across(f):
        if f == 0:
            return {"axial": jnp.maximum(k - 1, 0)}
        if f == 1:
            return {"axial": jnp.minimum(k + 1, rows - 1)}
        return {"circ": lax.rem(c + (cols - 1 if f == 2 else 1), cols)}

    def face_copy(out, into, send, recv, t, f):
        return pltpu.make_async_remote_copy(
            src_ref=out.at[t, f],
            dst_ref=into.at[t, f ^ 1],
            send_sem=send.at[t, f],
            recv_sem=recv.at[t, f ^ 1],
            device_id=across(f),
            device_id_type=MESH,
        )

    def guarded(f, action):
        if f < 2:
            pl.when(has[f])(action)
        else:
            action()

    def send_face(args, t, f):
        guarded(f, lambda: face_copy(*args, t, f).start())

    def wait_face(args, t, f):
        guarded(f, lambda: face_copy(*args, t, f ^ 1).wait_recv())

    def done_face(args, t, f):
        guarded(f, lambda: face_copy(*args, t, f).wait_send())

    halo = (hout, hin, hs, hr)
    tiles = (tile_out, tile_in, ts, tr)

    for f in range(2):

        @pl.when(jnp.logical_not(has[f]))
        def _():
            tile_in[0, f] = jnp.zeros(tile_in.shape[2:], F32)
            for t in range(GROUPS * HALOS):
                hin[t, f] = jnp.zeros(hin.shape[2:], F32)

    sub = lax.broadcasted_iota(jnp.int32, (width, width), 0)
    lane = lax.broadcasted_iota(jnp.int32, (width, width), 1)
    list_sub = lax.broadcasted_iota(jnp.int32, (width, list_len), 0)

    low_lanes = lane[:fold_rows] < fold_rows
    low8 = lane[:8] < fold_rows

    def roll(value):
        return pltpu.roll(value, fold_rows, 1)

    def spread(column):
        shape = (fold_rows, width)
        first = jnp.broadcast_to(column[:fold_rows], shape)
        return jnp.where(low_lanes, first, jnp.broadcast_to(column[fold_rows:], shape))

    def pick(f):
        return perm[f].astype(F32)

    for i in (9, 1, 2, 10, 0):
        arrivals[i].wait()

    for f in range(4):
        span = pl.ds(f * width, width)
        one = (order_ref[0, :, span] - f * width == sub).astype(F32)
        perm[f] = one.astype(BF16)
        rho = jnp.sum(one * rho_ref[0, :, span], axis=1, keepdims=True)
        dia = jnp.sum(one * diag_ref[0, :, span], axis=1, keepdims=True)
        diag[f] = spread(dia)
        share[f] = spread(rho)
        member = []
        for i in range(2):
            named = (lists_ref[0, 0, pl.ds(2 * f + i, 1), :] - f * width == list_sub).astype(F32)
            member.append(jnp.sum(named, axis=1, keepdims=True))
        pair = jnp.where(lane == 0, member[0], jnp.where(lane == 1, member[1], 0.0))
        pair = dot16(one.astype(BF16), pair.astype(BF16)) / list_len
        mean[2 * f] = spread(pair[:, 0:1])
        mean[2 * f + 1] = spread(pair[:, 1:2])
        packed = jnp.where(
            lane == 0, rho, jnp.where(lane == 1, pair[:, 0:1], jnp.where(lane == 2, pair[:, 1:2], 0.0))
        )
        tile_out[0, f] = packed.T[0:8]
        whole = lax.dot_general(
            one,
            load_ref[0, 0, :, span],
            NT,
            precision=lax.Precision.HIGHEST,
            preferred_element_type=F32,
        )
        top, bottom = whole[:fold_rows], whole[fold_rows:]
        hout[0, f] = jnp.where(low_lanes, top, roll(bottom))
        hout[1, f] = jnp.where(low_lanes, roll(top), bottom)

    pl.semaphore_wait(barrier, rows + cols - 2)
    for f in (2, 3, 0, 1):
        send_face(tiles, 0, f)
    for g in range(GROUPS):
        for f in (2, 3, 0, 1):
            send_face(halo, g, f)

    for i in (7, 8, 6):
        arrivals[i].wait()

    small_sub = lax.broadcasted_iota(jnp.int32, (8, 8), 0)
    small_lane = lax.broadcasted_iota(jnp.int32, (8, 8), 1)
    for i, ref in enumerate((lower_ref, upper_ref)):
        column = jnp.sum(jnp.where(small_sub == small_lane, ref[...], 0.0), axis=1, keepdims=True)
        coef_in[k, i] = jnp.broadcast_to(column, (8, width))

    def coef_copy(d):
        return pltpu.make_async_remote_copy(
            src_ref=coef_in.at[k],
            dst_ref=coef_in.at[k],
            send_sem=fs.at[d],
            recv_sem=fr.at[d],
            device_id=axial_peer(d),
            device_id_type=MESH,
        )

    def coef_arrival(d):
        row = lax.rem(k + rows - d, rows)
        return pltpu.make_async_remote_copy(
            src_ref=coef_in.at[row],
            dst_ref=coef_in.at[row],
            send_sem=fs.at[d],
            recv_sem=fr.at[d],
            device_id=axial_peer(d),
            device_id_type=MESH,
        )

    for d in range(1, rows):
        coef_copy(d).start()

    for f in (0, 1, 2, 3):
        wait_face(tiles, 0, f)
        got = jnp.concatenate([tile_in[0, f], jnp.zeros((width - 8, width), F32)], axis=0).T
        mine = share[f]
        theirs = spread(got[:, 0:1])
        both = mine + theirs
        own_share = mine / both
        near_share = theirs / both
        share[f] = own_share
        masked = own_share * keep[f] if f < 2 else own_share
        for i in range(2):
            own_w[2 * f + i] = masked * mean[2 * f + i]
            near_w[2 * f + i] = near_share * spread(got[:, 1 + i : 2 + i])

    def circ_copy(t, d):
        return pltpu.make_async_remote_copy(
            src_ref=c_out.at[t],
            dst_ref=c_in.at[t, d],
            send_sem=cs.at[t, d],
            recv_sem=cr.at[t, d],
            device_id=circ_peer(d),
            device_id_type=MESH,
        )

    def axial_copy(t, d, row):
        return pltpu.make_async_remote_copy(
            src_ref=a_in.at[t, row],
            dst_ref=a_in.at[t, row],
            send_sem=as_.at[t, d],
            recv_sem=ar.at[t, d],
            device_id=axial_peer(d),
            device_id_type=MESH,
        )

    def sum_begin(t, value):
        c_out[t] = value
        for d in range(1, cols):
            circ_copy(t, d).start()

    def sum_middle(t):
        value = c_out[t]
        for d in range(1, cols):
            circ_copy(t, d).wait_recv()
            value = value + c_in[t, d]
        a_in[t, k] = value
        for d in range(1, rows):
            axial_copy(t, d, k).start()

    def sum_end(t):
        for d in range(1, rows):
            axial_copy(t, d, lax.rem(k + rows - d, rows)).wait_recv()

    def dot_total(t, row):
        value = a_in[t, 0, pl.ds(row, 1)]
        for m in range(1, rows):
            value = value + a_in[t, m, pl.ds(row, 1)]
        return jnp.where(low8[:1], roll(value), value)

    sub8 = lax.broadcasted_iota(jnp.int32, (8, width), 0)

    def packed_tile(first, second):
        zero = jnp.zeros((1, width), F32)
        second = jnp.concatenate(second + [zero] * (8 - len(second)), axis=0)
        second = second + roll(second)
        if first is None:
            return second
        first = jnp.concatenate(first, axis=0)
        return jnp.where(low8, first + roll(first), second)

    def fold(value):
        return jnp.sum(value, axis=0, keepdims=True)

    def constraint_tile(field, dots):
        first = []
        for q in range(8):
            value = own_w[q] * field(q // 2)
            if q in (4, 5):
                value = value + near_w[q + 2] * field(3)
            if q in (6, 7):
                value = value + near_w[q - 2] * field(2)
            first.append(fold(value))
        second = [fold(near_w[i] * field(i // 2)) for i in (2, 3, 0, 1)]
        return packed_tile(first, second + dots)

    def row_totals(t, m):
        value = a_in[t, m]
        value = jnp.where(low8, value, roll(value))
        if m > 0:
            other = a_in[t, m - 1]
            other = jnp.where(low8, roll(other), other)
            value = value + jnp.where(sub8 < 2, other, 0.0)
        if m < rows - 1:
            other = a_in[t, m + 1]
            other = jnp.where(low8, roll(other), other)
            value = value + jnp.where(jnp.logical_and(sub8 >= 2, sub8 < 4), other, 0.0)
        return value

    for g in range(GROUPS):
        sum_begin(g, constraint_tile(lambda f: hout[g, f], []))

    arrivals[5].wait()

    def store_pair(table, f, cut, value):
        high, low = split(value)
        table[f, pl.ds(0, width), cut] = high
        table[f, pl.ds(width, width), cut] = low

    for f in range(4):
        rows_f = pl.ds(f * width, width)
        high, low = split(neumann_ref[0, 0, rows_f, :])
        high = dot16(perm[f], high).astype(BF16)
        low = dot16(perm[f], low).astype(BF16)
        for g in range(4):
            cut = slice(g * width, (g + 1) * width)
            span = pl.ds(g * width, width)
            neumann[f, pl.ds(0, width), span] = dot16(high[:, cut], perm[g], NT).astype(BF16)
            neumann[f, pl.ds(width, width), span] = dot16(low[:, cut], perm[g], NT).astype(BF16)

    for g in range(GROUPS):
        sum_middle(g)

    def apply(table, g, field):
        for f in range(4):
            value = field(f)
            high = value.astype(BF16).astype(F32)
            low = value - high
            top = jnp.where(low_lanes, high, roll(low))
            bottom = jnp.where(low_lanes, roll(high), low)
            vbuf[g, pl.ds(f * width, fold_rows), :] = top.astype(BF16)
            vbuf[g, pl.ds(f * width + fold_rows, fold_rows), :] = bottom.astype(BF16)

        def one(f):
            full = dot16(table[f], vbuf[g])
            full = full[:width] + full[width:]
            top, bottom = full[:fold_rows], full[fold_rows:]
            return jnp.where(low_lanes, top, bottom) + roll(jnp.where(low_lanes, bottom, top))

        return one

    def assembled(t, f):
        value = hout[t, f] + hin[t, f]
        return value * keep[f] if f < 2 else value

    def coarse_value(g):
        smooth = []
        h = jnp.zeros((8, width), F32)
        for m in range(rows):
            factor = coef_in[m, 0]
            h = factor * h + (1.0 - factor) * totals[g, m]
            smooth.append(h)
        top = jnp.zeros((8, width), F32)
        mine = jnp.zeros((8, width), F32)
        for m in reversed(range(rows)):
            factor = coef_in[m, 1]
            top = factor * top + (1.0 - factor) * smooth[m]
            mine = mine + jnp.where(k == m, top, 0.0)
        own = totals[g, k]
        for q in range(8):
            mine = mine + coarse_ref[0, :, pl.ds(q, 1)] * own[q : q + 1]
        return mine

    def precondition(t, g):
        local = apply(neumann, g, lambda f: share[f] * r[g, f])
        coarse = coarse_value(g)
        for f in (2, 3, 0, 1):
            value = local(f)
            for i in range(2):
                q = 2 * f + i
                value = value + mean[q] * coarse[q : q + 1]
            value = share[f] * value
            hout[GROUPS * t + g, f] = value
            send_face(halo, GROUPS * t + g, f)

    for g in range(GROUPS):
        for f in (0, 1, 2, 3):
            wait_face(halo, g, f)
            r[g, f] = assembled(g, f)
        sum_end(g)
        if g == 0:
            for d in range(1, rows):
                coef_arrival(d).wait_recv()
        for m in range(rows):
            totals[g, m] = row_totals(g, m)
        precondition(1, g)

    arrivals[3].wait()
    arrivals[4].wait()

    for f in range(4):
        span = pl.ds(f * width, width)
        high, low = split(couple_ref[0, 0, span, :])
        half[0, span, :] = dot16(perm[f], high).astype(BF16)
        half[1, span, :] = dot16(perm[f], low).astype(BF16)
    for n in range(blocks_ref.shape[2]):
        cut = pl.ds(n * block, block)
        ih, il = split(blocks_ref[0, 0, n])
        ch, cl = half[0, :, cut], half[1, :, cut]
        high, low = split(dot16(ch, ih) + (dot16(ch, il) + dot16(cl, ih)))
        half[2, :, cut] = high
        half[3, :, cut] = low
    for f in range(4):
        span = pl.ds(f * width, width)
        eh, el = half[2, span, :], half[3, span, :]
        ch, cl = half[0], half[1]
        value = dot16(eh, ch, NT) + (dot16(eh, cl, NT) + dot16(el, ch, NT))
        store_pair(schur, f, slice(None), value)

    rz = [None] * GROUPS
    pap = [None] * GROUPS
    for step in range(ITERS):
        last = step + 1 == ITERS
        for g in range(GROUPS):
            t = GROUPS * (1 + 2 * step) + g
            u = t + GROUPS
            s = GROUPS * (step + 1) + g
            for f in (0, 1, 2, 3):
                wait_face(halo, t, f)
            back = apply(schur, g, lambda f: assembled(t, f))
            dots = [jnp.zeros((1, width), F32) for _ in range(2 if step == 0 else 3)]
            for f in (2, 3, 0, 1):
                z = assembled(t, f)
                value = diag[f] * z - back(f)
                hout[u, f] = value
                dots[0] = dots[0] + fold(0.5 * (r[g, f] * z))
                dots[1] = dots[1] + fold(z * value)
                if step > 0:
                    dots[2] = dots[2] + fold(0.5 * (z * image[g, f]) + p[g, f] * value)
            if last:
                sum_begin(s, packed_tile(None, [jnp.zeros((1, width), F32)] * 4 + dots))
            else:
                sum_begin(s, constraint_tile(lambda f: hout[u, f], dots))
            for f in (2, 3, 0, 1):
                send_face(halo, u, f)
        for g in range(GROUPS):
            sum_middle(GROUPS * (step + 1) + g)
        for g in range(GROUPS):
            t = GROUPS * (1 + 2 * step) + g
            u = t + GROUPS
            s = GROUPS * (step + 1) + g
            for f in (0, 1, 2, 3):
                wait_face(halo, u, f)
            sum_end(s)
            new = dot_total(s, 4)
            new_pap = dot_total(s, 5)
            if step > 0:
                beta = new / rz[g]
                new_pap = new_pap + beta * (dot_total(s, 6) + beta * pap[g])
            rz[g], pap[g] = new, new_pap
            alpha = new / new_pap
            for f in range(4):
                z = assembled(t, f)
                w = assembled(u, f)
                if step > 0:
                    z = z + beta * p[g, f]
                    w = w + beta * image[g, f]
                p[g, f] = z
                image[g, f] = w
                x[g, f] = alpha * z if step == 0 else x[g, f] + alpha * z
                r[g, f] = r[g, f] - alpha * w
            if not last:
                for m in range(rows):
                    value = row_totals(s, m)
                    if step > 0:
                        value = value + beta * moved[g, m]
                    moved[g, m] = value
                    totals[g, m] = totals[g, m] - alpha * value
                precondition(1 + 2 * (step + 1), g)

    for f in range(4):
        span = pl.ds(f * width, width)
        one = pick(f)
        for ref, field in ((x_out, x), (r_out, r)):
            first, second = field[0, f], field[1, f]
            top = jnp.where(low_lanes, first, roll(second))
            bottom = jnp.where(low_lanes, roll(first), second)
            ref[0, 0, :, span] = jnp.dot(
                jnp.concatenate([top, bottom], axis=0).T, one, precision=lax.Precision.HIGHEST, preferred_element_type=F32
            )

    for f in range(4):
        done_face(tiles, 0, f)
        for t in range(GROUPS * HALOS):
            done_face(halo, t, f)
    for d in range(1, rows):
        coef_copy(d).wait_send()
    for t in range(GROUPS * SUMS):
        for d in range(1, cols):
            circ_copy(t, d).wait_send()
        for d in range(1, rows):
            axial_copy(t, d, k).wait_send()


def local(rows, cols, *args):
    load = args[0]
    count, points = load.shape[2:]
    width = points // 4
    dma = pltpu.SemaphoreType.DMA
    half = (4, width // GROUPS, width)
    halos, sums = GROUPS * HALOS, GROUPS * SUMS
    scratch = [pltpu.VMEM(arg.shape, arg.dtype) for arg in args] + [
        dma((len(args),)),
        pltpu.VMEM((halos,) + half, F32),
        pltpu.VMEM((halos,) + half, F32),
        pltpu.VMEM((1, 4, 8, width), F32),
        pltpu.VMEM((1, 4, 8, width), F32),
        pltpu.VMEM((sums, 8, width), F32),
        pltpu.VMEM((sums, cols, 8, width), F32),
        pltpu.VMEM((sums, rows, 8, width), F32),
        pltpu.VMEM((rows, 2, 8, width), F32),
        pltpu.VMEM((4, width, width), BF16),
        pltpu.VMEM((4, 2 * width, points), BF16),
        pltpu.VMEM((4, 2 * width, points), BF16),
        pltpu.VMEM((4, points, args[3].shape[-1]), BF16),
        pltpu.VMEM((GROUPS, points, width), BF16),
        pltpu.VMEM(half, F32),
        pltpu.VMEM(half, F32),
        pltpu.VMEM((8,) + half[1:], F32),
        pltpu.VMEM((8,) + half[1:], F32),
        pltpu.VMEM((8,) + half[1:], F32),
        pltpu.VMEM((GROUPS,) + half, F32),
        pltpu.VMEM((GROUPS,) + half, F32),
        pltpu.VMEM((GROUPS,) + half, F32),
        pltpu.VMEM((GROUPS,) + half, F32),
        pltpu.VMEM((GROUPS, rows, 8, width), F32),
        pltpu.VMEM((GROUPS, rows, 8, width), F32),
        dma((halos, 4)),
        dma((halos, 4)),
        dma((1, 4)),
        dma((1, 4)),
        dma((sums, cols)),
        dma((sums, cols)),
        dma((sums, rows)),
        dma((sums, rows)),
        dma((rows,)),
        dma((rows,)),
    ]
    shape = jax.ShapeDtypeStruct(load.shape, F32)
    return pl.pallas_call(
        functools.partial(kernel, rows, cols),
        out_shape=(shape, shape),
        in_specs=[pl.BlockSpec(memory_space=pl.ANY)] * len(args),
        out_specs=(pl.BlockSpec(memory_space=pltpu.VMEM),) * 2,
        scratch_shapes=scratch,
        compiler_params=pltpu.CompilerParams(
            collective_id=0, has_side_effects=True, vmem_limit_bytes=56 * 2**20
        ),
    )(*args)


def solution(mesh):
    in_specs = (
        P("axial", "circ", None, None),
        P("axial", "circ", None),
        P("axial", "circ", None),
        P("axial", "circ", None, None),
        P("axial", "circ", None, None, None),
        P("axial", "circ", None, None),
        P("axial", None, None),
        P("axial", None),
        P("axial", None),
        P("axial", "circ", None),
        P("axial", "circ", None, None),
    )
    out_specs = (P("axial", "circ", None, None), P("axial", "circ", None, None))
    body = functools.partial(local, mesh.shape["axial"], mesh.shape["circ"])
    return jax.shard_map(body, mesh=mesh, in_specs=in_specs, out_specs=out_specs, check_vma=False)
```

```python
import functools

import jax
import jax.numpy as jnp
from jax import lax
from jax.experimental import pallas as pl
from jax.experimental.pallas import tpu as pltpu
from jax.sharding import PartitionSpec as P

ITERS = 3
F32 = jnp.float32
BF16 = jnp.bfloat16
MESH = pl.DeviceIdType.MESH
NT = (((1,), (1,)), ((), ()))
HALOS = 1 + 2 * ITERS
SUMS = 1 + ITERS


def split(value):
    high = value.astype(BF16)
    return high, (value - high.astype(F32)).astype(BF16)


def split3(value):
    high = value.astype(BF16)
    rest = value - high.astype(F32)
    middle = rest.astype(BF16)
    return high, middle, (rest - middle.astype(F32)).astype(BF16)


def dot16(a, b, dims=(((1,), (0,)), ((), ()))):
    return lax.dot_general(a, b, dims, preferred_element_type=F32)


def kernel(
    rows,
    cols,
    *refs,
):
    sources, refs = refs[:11], refs[11:]
    (x_out, r_out), refs = refs[:2], refs[2:]
    held, in_sem, refs = refs[:11], refs[11], refs[12:]
    (
        load_ref, rho_ref, diag_ref, couple_ref, blocks_ref, neumann_ref,
        coarse_ref, lower_ref, upper_ref, order_ref, lists_ref,
    ) = held
    (
        hout, hin, tile_out, tile_in, c_out, c_in, a_in, coef_in, perm, schur, neumann, half, vbuf, wide, wide_t, inner, turned,
        share, diag, mean, own_w, near_w, x, r, p, image, totals, moved,
        hs, hr, ts, tr, cs, cr, as_, ar, fs, fr,
    ) = refs
    k = lax.axis_index("axial")
    c = lax.axis_index("circ")
    width = perm.shape[1]
    arrivals = [
        pltpu.make_async_copy(source, target, in_sem.at[i])
        for i, (source, target) in enumerate(zip(sources, held))
    ]
    for i in (9, 1, 2, 10, 0, 7, 8, 6, 5, 3, 4):
        arrivals[i].start()
    block = blocks_ref.shape[-1]
    list_len = lists_ref.shape[-1]

    def circ_peer(d):
        return {"circ": lax.rem(c + d, cols)}

    def axial_peer(d):
        return {"axial": lax.rem(k + d, rows)}

    barrier = pltpu.get_barrier_semaphore()
    for d in range(1, cols):
        pl.semaphore_signal(barrier, inc=1, device_id=circ_peer(d), device_id_type=MESH)
    for d in range(1, rows):
        pl.semaphore_signal(barrier, inc=1, device_id=axial_peer(d), device_id_type=MESH)

    has = (k > 0, k < rows - 1)
    keep = [has[0].astype(F32), has[1].astype(F32)]

    def across(f):
        if f == 0:
            return {"axial": jnp.maximum(k - 1, 0)}
        if f == 1:
            return {"axial": jnp.minimum(k + 1, rows - 1)}
        return {"circ": lax.rem(c + (cols - 1 if f == 2 else 1), cols)}

    def face_copy(out, into, send, recv, t, f):
        return pltpu.make_async_remote_copy(
            src_ref=out.at[t, f],
            dst_ref=into.at[t, f ^ 1],
            send_sem=send.at[t, f],
            recv_sem=recv.at[t, f ^ 1],
            device_id=across(f),
            device_id_type=MESH,
        )

    def guarded(f, action):
        if f < 2:
            pl.when(has[f])(action)
        else:
            action()

    def send_face(args, t, f):
        guarded(f, lambda: face_copy(*args, t, f).start())

    def wait_face(args, t, f):
        guarded(f, lambda: face_copy(*args, t, f ^ 1).wait_recv())

    def done_face(args, t, f):
        guarded(f, lambda: face_copy(*args, t, f).wait_send())

    halo = (hout, hin, hs, hr)
    tiles = (tile_out, tile_in, ts, tr)

    for f in range(2):

        @pl.when(jnp.logical_not(has[f]))
        def _():
            tile_in[0, f] = jnp.zeros(tile_in.shape[2:], F32)
            for t in range(HALOS):
                hin[t, f] = jnp.zeros(hin.shape[2:], F32)

    sub = lax.broadcasted_iota(jnp.int32, (width, width), 0)
    lane = lax.broadcasted_iota(jnp.int32, (width, width), 1)
    list_sub = lax.broadcasted_iota(jnp.int32, (width, list_len), 0)

    def spread(column):
        return jnp.broadcast_to(column, (width, width))

    for i in (9, 1, 2, 10, 0):
        arrivals[i].wait()

    wide[...] = jnp.zeros_like(wide)
    wide_t[...] = jnp.zeros_like(wide_t)
    inner[...] = jnp.zeros_like(inner)

    for f in range(4):
        span = pl.ds(f * width, width)
        one = (order_ref[0, :, span] - f * width == sub).astype(F32)
        perm[f] = one.astype(BF16)
        corner = pl.ds((f % 2) * width, width)
        wide[f // 2, corner, corner] = one.astype(BF16)
        wide_t[f // 2, corner, corner] = one.T.astype(BF16)
        rho = jnp.sum(one * rho_ref[0, :, span], axis=1, keepdims=True)
        dia = jnp.sum(one * diag_ref[0, :, span], axis=1, keepdims=True)
        diag[f] = spread(dia)
        share[f] = spread(rho)
        member = []
        for i in range(2):
            named = (lists_ref[0, 0, pl.ds(2 * f + i, 1), :] - f * width == list_sub).astype(F32)
            member.append(jnp.sum(named, axis=1, keepdims=True))
        pair = jnp.where(lane == 0, member[0], jnp.where(lane == 1, member[1], 0.0))
        pair = dot16(one.astype(BF16), pair.astype(BF16)) / list_len
        mean[2 * f] = spread(pair[:, 0:1])
        mean[2 * f + 1] = spread(pair[:, 1:2])
        packed = jnp.where(
            lane == 0, rho, jnp.where(lane == 1, pair[:, 0:1], jnp.where(lane == 2, pair[:, 1:2], 0.0))
        )
        tile_out[0, f] = packed.T[0:8]
        full = dot16(perm[f], jnp.concatenate(split3(load_ref[0, 0, :, span].T), axis=1))
        tail = full[:, width : 2 * width] + full[:, 2 * width :]
        hout[0, f] = full[:, :width] + tail

    pl.semaphore_wait(barrier, rows + cols - 2)
    for f in (2, 3, 0, 1):
        send_face(tiles, 0, f)
    for f in (2, 3, 0, 1):
        send_face(halo, 0, f)

    for i in (7, 8, 6):
        arrivals[i].wait()

    small_sub = lax.broadcasted_iota(jnp.int32, (8, 8), 0)
    small_lane = lax.broadcasted_iota(jnp.int32, (8, 8), 1)
    for i, ref in enumerate((lower_ref, upper_ref)):
        column = jnp.sum(jnp.where(small_sub == small_lane, ref[...], 0.0), axis=1, keepdims=True)
        coef_in[k, i] = jnp.broadcast_to(column, (8, width))

    def coef_copy(d):
        return pltpu.make_async_remote_copy(
            src_ref=coef_in.at[k],
            dst_ref=coef_in.at[k],
            send_sem=fs.at[d],
            recv_sem=fr.at[d],
            device_id=axial_peer(d),
            device_id_type=MESH,
        )

    def coef_arrival(d):
        row = lax.rem(k + rows - d, rows)
        return pltpu.make_async_remote_copy(
            src_ref=coef_in.at[row],
            dst_ref=coef_in.at[row],
            send_sem=fs.at[d],
            recv_sem=fr.at[d],
            device_id=axial_peer(d),
            device_id_type=MESH,
        )

    for d in range(1, rows):
        coef_copy(d).start()

    for f in (0, 1, 2, 3):
        wait_face(tiles, 0, f)
        got = jnp.concatenate([tile_in[0, f], jnp.zeros((width - 8, width), F32)], axis=0).T
        mine = share[f]
        theirs = spread(got[:, 0:1])
        both = mine + theirs
        own_share = mine / both
        near_share = theirs / both
        share[f] = own_share
        masked = own_share * keep[f] if f < 2 else own_share
        for i in range(2):
            own_w[2 * f + i] = masked * mean[2 * f + i]
            near_w[2 * f + i] = near_share * spread(got[:, 1 + i : 2 + i])

    def span_of(t):
        return pl.ds(8, 8) if t == ITERS else pl.ds(0, 16)

    def circ_copy(t, d):
        return pltpu.make_async_remote_copy(
            src_ref=c_out.at[t, span_of(t)],
            dst_ref=c_in.at[t, d, span_of(t)],
            send_sem=cs.at[t, d],
            recv_sem=cr.at[t, d],
            device_id=circ_peer(d),
            device_id_type=MESH,
        )

    def axial_copy(t, d, row):
        return pltpu.make_async_remote_copy(
            src_ref=a_in.at[t, row, span_of(t)],
            dst_ref=a_in.at[t, row, span_of(t)],
            send_sem=as_.at[t, d],
            recv_sem=ar.at[t, d],
            device_id=axial_peer(d),
            device_id_type=MESH,
        )

    def sum_begin(t, value):
        c_out[t, span_of(t)] = value
        for d in range(1, cols):
            circ_copy(t, d).start()

    def sum_middle(t):
        value = c_out[t, span_of(t)]
        for d in range(1, cols):
            circ_copy(t, d).wait_recv()
            value = value + c_in[t, d, span_of(t)]
        a_in[t, k, span_of(t)] = value
        for d in range(1, rows):
            axial_copy(t, d, k).start()

    def sum_end(t):
        for d in range(1, rows):
            axial_copy(t, d, lax.rem(k + rows - d, rows)).wait_recv()

    def dot_total(t, row):
        value = a_in[t, 0, pl.ds(row, 1)]
        for m in range(1, rows):
            value = value + a_in[t, m, pl.ds(row, 1)]
        return value

    sub8 = lax.broadcasted_iota(jnp.int32, (8, width), 0)

    def dot_tile(dots, head):
        dots = dots + [jnp.zeros((1, width), F32)] * (4 - len(dots))
        return jnp.concatenate(head + dots, axis=0)

    def constraint_tiles(field, dots):
        def one(table, index, f):
            return jnp.sum(table[index] * field(f), axis=0, keepdims=True)

        first = []
        for q in range(8):
            value = own_w[q] * field(q // 2)
            if q in (4, 5):
                value = value + near_w[q + 2] * field(3)
            if q in (6, 7):
                value = value + near_w[q - 2] * field(2)
            first.append(jnp.sum(value, axis=0, keepdims=True))
        second = [one(near_w, 2, 1), one(near_w, 3, 1), one(near_w, 0, 0), one(near_w, 1, 0)]
        return dot_tile(dots, first + second)

    def row_totals(t, m):
        value = a_in[t, m, pl.ds(0, 8)]
        if m > 0:
            value = value + jnp.where(sub8 < 2, a_in[t, m - 1, pl.ds(8, 8)], 0.0)
        if m < rows - 1:
            value = value + jnp.where(
                jnp.logical_and(sub8 >= 2, sub8 < 4), a_in[t, m + 1, pl.ds(8, 8)], 0.0
            )
        return value

    sum_begin(0, constraint_tiles(lambda f: hout[0, f], []))

    arrivals[5].wait()

    def store_pair(table, f, cut, value):
        high, low = split(value)
        table[f, pl.ds(0, width), cut] = high
        table[f, pl.ds(width, width), cut] = low

    points = 4 * width
    pair = 2 * width
    high, low = split(neumann_ref[0, 0])
    for a in range(2):
        cut = slice(a * pair, (a + 1) * pair)
        for i, part in enumerate((high, low)):
            turned[pl.ds(i * points, points), pl.ds(a * pair, pair)] = dot16(
                part[:, cut], wide_t[a]
            ).astype(BF16)
    for a in range(2):
        for i in range(2):
            done = dot16(wide[a], turned[pl.ds(i * points + a * pair, pair), :]).astype(BF16)
            for j in range(2):
                neumann[2 * a + j, pl.ds(i * width, width), :] = done[j * width : (j + 1) * width]

    sum_middle(0)

    def apply(table, field):
        for f in range(4):
            high, low = split(field(f))
            vbuf[pl.ds(f * width, width), pl.ds(0, width)] = high
            vbuf[pl.ds(f * width, width), pl.ds(width, width)] = low

        def one(f):
            full = dot16(table[f], vbuf[...])
            small = full[:width, width:] + full[width:, :width] + full[width:, width:]
            return full[:width, :width] + small

        return one

    def assembled(t, f):
        value = hout[t, f] + hin[t, f]
        return value * keep[f] if f < 2 else value

    def coarse_value():
        smooth = []
        h = jnp.zeros((8, width), F32)
        for m in range(rows):
            factor = coef_in[m, 0]
            h = factor * h + (1.0 - factor) * totals[m]
            smooth.append(h)
        top = jnp.zeros((8, width), F32)
        mine = jnp.zeros((8, width), F32)
        for m in reversed(range(rows)):
            factor = coef_in[m, 1]
            top = factor * top + (1.0 - factor) * smooth[m]
            mine = mine + jnp.where(k == m, top, 0.0)
        own = totals[k]
        for q in range(8):
            mine = mine + coarse_ref[0, :, pl.ds(q, 1)] * own[q : q + 1]
        return mine

    def precondition(t):
        local = apply(neumann, lambda f: share[f] * r[f])
        coarse = coarse_value()
        for f in (2, 3, 0, 1):
            value = local(f)
            for i in range(2):
                q = 2 * f + i
                value = value + mean[q] * coarse[q : q + 1]
            value = share[f] * value
            hout[t, f] = value
            send_face(halo, t, f)

    for f in (0, 1, 2, 3):
        wait_face(halo, 0, f)
        r[f] = assembled(0, f)
    sum_end(0)
    for d in range(1, rows):
        coef_arrival(d).wait_recv()
    for m in range(rows):
        totals[m] = row_totals(0, m)
    precondition(1)

    arrivals[3].wait()
    arrivals[4].wait()

    high, low = split(couple_ref[0, 0])
    for a in range(2):
        cut = slice(a * pair, (a + 1) * pair)
        for i, part in enumerate((high, low)):
            half[i, pl.ds(a * pair, pair), :] = dot16(wide[a], part[cut]).astype(BF16)
    for n in range(blocks_ref.shape[2]):
        corner = pl.ds((n % 2) * block, block)
        for i, part in enumerate(split(blocks_ref[0, 0, n])):
            inner[i, n // 2, corner, corner] = part
    for a in range(2):
        cut = pl.ds(a * pair, pair)
        ch, cl = half[0, :, cut], half[1, :, cut]
        ih, il = inner[0, a], inner[1, a]
        high, low = split(dot16(ch, ih) + (dot16(ch, il) + dot16(cl, ih)))
        half[2, :, cut] = high
        half[3, :, cut] = low
    both = dot16(half[pl.ds(2, 2)].reshape(2 * points, points), half[0], NT)
    value = both[:points] + (both[points:] + dot16(half[2], half[1], NT))
    for f in range(4):
        store_pair(schur, f, slice(None), value[f * width : (f + 1) * width])

    def fold(value):
        return jnp.sum(value, axis=0, keepdims=True)

    rz = None
    pap = None
    for step in range(ITERS):
        t = 1 + 2 * step
        last = step + 1 == ITERS
        for f in (0, 1, 2, 3):
            wait_face(halo, t, f)
        back = apply(schur, lambda f: assembled(t, f))
        dots = [jnp.zeros((1, width), F32) for _ in range(2 if step == 0 else 3)]
        for f in (2, 3, 0, 1):
            z = assembled(t, f)
            value = diag[f] * z - back(f)
            hout[t + 1, f] = value
            dots[0] = dots[0] + 0.5 * fold(r[f] * z)
            dots[1] = dots[1] + fold(z * value)
            if step > 0:
                dots[2] = dots[2] + fold(0.5 * (z * image[f]) + p[f] * value)
        if last:
            sum_begin(step + 1, dot_tile(dots, [jnp.zeros((1, width), F32)] * 4))
        else:
            sum_begin(step + 1, constraint_tiles(lambda f: hout[t + 1, f], dots))
        for f in (2, 3, 0, 1):
            send_face(halo, t + 1, f)
        sum_middle(step + 1)
        for f in (0, 1, 2, 3):
            wait_face(halo, t + 1, f)
        sum_end(step + 1)
        new = dot_total(step + 1, 12)
        new_pap = dot_total(step + 1, 13)
        if step > 0:
            beta = new / rz
            new_pap = new_pap + beta * (dot_total(step + 1, 14) + beta * pap)
        rz, pap = new, new_pap
        alpha = rz / pap
        for f in range(4):
            z = assembled(t, f)
            w = assembled(t + 1, f)
            if step > 0:
                z = z + beta * p[f]
                w = w + beta * image[f]
            p[f] = z
            image[f] = w
            x[f] = alpha * z if step == 0 else x[f] + alpha * z
            r[f] = r[f] - alpha * w
        if not last:
            for m in range(rows):
                value = row_totals(step + 1, m)
                if step > 0:
                    value = value + beta * moved[m]
                moved[m] = value
                totals[m] = totals[m] - alpha * value
            precondition(t + 2)

    for f in range(4):
        span = pl.ds(f * width, width)
        parts = split3(x[f].T) + split3(r[f].T)
        full = dot16(jnp.concatenate(parts, axis=0), perm[f])
        full = [full[i * width : (i + 1) * width] for i in range(6)]
        x_out[0, 0, :, span] = full[0] + (full[1] + full[2])
        r_out[0, 0, :, span] = full[3] + (full[4] + full[5])

    for f in range(4):
        done_face(tiles, 0, f)
        for t in range(HALOS):
            done_face(halo, t, f)
    for d in range(1, rows):
        coef_copy(d).wait_send()
    for t in range(SUMS):
        for d in range(1, cols):
            circ_copy(t, d).wait_send()
        for d in range(1, rows):
            axial_copy(t, d, k).wait_send()


def local(rows, cols, *args):
    load = args[0]
    count, points = load.shape[2:]
    width = points // 4
    dma = pltpu.SemaphoreType.DMA
    face = (4, width, width)
    scratch = [pltpu.VMEM(arg.shape, arg.dtype) for arg in args] + [
        dma((len(args),)),
        pltpu.VMEM((HALOS,) + face, F32),
        pltpu.VMEM((HALOS,) + face, F32),
        pltpu.VMEM((1, 4, 8, width), F32),
        pltpu.VMEM((1, 4, 8, width), F32),
        pltpu.VMEM((SUMS, 16, width), F32),
        pltpu.VMEM((SUMS, cols, 16, width), F32),
        pltpu.VMEM((SUMS, rows, 16, width), F32),
        pltpu.VMEM((rows, 2, 8, width), F32),
        pltpu.VMEM(face, BF16),
        pltpu.VMEM((4, 2 * width, points), BF16),
        pltpu.VMEM((4, 2 * width, points), BF16),
        pltpu.VMEM((4, points, args[3].shape[-1]), BF16),
        pltpu.VMEM((points, 2 * width), BF16),
        pltpu.VMEM((2, 2 * width, 2 * width), BF16),
        pltpu.VMEM((2, 2 * width, 2 * width), BF16),
        pltpu.VMEM((2, 2, 2 * width, 2 * width), BF16),
        pltpu.VMEM((2 * points, points), BF16),
        pltpu.VMEM(face, F32),
        pltpu.VMEM(face, F32),
        pltpu.VMEM((8, width, width), F32),
        pltpu.VMEM((8, width, width), F32),
        pltpu.VMEM((8, width, width), F32),
        pltpu.VMEM(face, F32),
        pltpu.VMEM(face, F32),
        pltpu.VMEM(face, F32),
        pltpu.VMEM(face, F32),
        pltpu.VMEM((rows, 8, width), F32),
        pltpu.VMEM((rows, 8, width), F32),
        dma((HALOS, 4)),
        dma((HALOS, 4)),
        dma((1, 4)),
        dma((1, 4)),
        dma((SUMS, cols)),
        dma((SUMS, cols)),
        dma((SUMS, rows)),
        dma((SUMS, rows)),
        dma((rows,)),
        dma((rows,)),
    ]
    shape = jax.ShapeDtypeStruct(load.shape, F32)
    return pl.pallas_call(
        functools.partial(kernel, rows, cols),
        out_shape=(shape, shape),
        in_specs=[pl.BlockSpec(memory_space=pl.ANY)] * len(args),
        out_specs=(pl.BlockSpec(memory_space=pltpu.VMEM),) * 2,
        scratch_shapes=scratch,
        compiler_params=pltpu.CompilerParams(
            collective_id=0, has_side_effects=True, vmem_limit_bytes=56 * 2**20
        ),
    )(*args)


def solution(mesh):
    in_specs = (
        P("axial", "circ", None, None),
        P("axial", "circ", None),
        P("axial", "circ", None),
        P("axial", "circ", None, None),
        P("axial", "circ", None, None, None),
        P("axial", "circ", None, None),
        P("axial", None, None),
        P("axial", None),
        P("axial", None),
        P("axial", "circ", None),
        P("axial", "circ", None, None),
    )
    out_specs = (P("axial", "circ", None, None), P("axial", "circ", None, None))
    body = functools.partial(local, mesh.shape["axial"], mesh.shape["circ"])
    return jax.shard_map(body, mesh=mesh, in_specs=in_specs, out_specs=out_specs, check_vma=False)
```

```python
import functools

import jax
import jax.numpy as jnp
from jax import lax
from jax.experimental import pallas as pl
from jax.experimental.pallas import tpu as pltpu
from jax.sharding import PartitionSpec as P

ITERS = 3
F32 = jnp.float32
BF16 = jnp.bfloat16
MESH = pl.DeviceIdType.MESH
NT = (((1,), (1,)), ((), ()))
HALOS = 1 + 2 * ITERS
SUMS = 1 + ITERS


def split(value):
    high = value.astype(BF16)
    return high, (value - high.astype(F32)).astype(BF16)


def split3(value):
    high = value.astype(BF16)
    rest = value - high.astype(F32)
    middle = rest.astype(BF16)
    return high, middle, (rest - middle.astype(F32)).astype(BF16)


def dot16(a, b, dims=(((1,), (0,)), ((), ()))):
    return lax.dot_general(a, b, dims, preferred_element_type=F32)


def kernel(
    rows,
    cols,
    *refs,
):
    sources, refs = refs[:11], refs[11:]
    (x_out, r_out), refs = refs[:2], refs[2:]
    held, in_sem, refs = refs[:11], refs[11], refs[12:]
    (
        load_ref, rho_ref, diag_ref, couple_ref, blocks_ref, neumann_ref,
        coarse_ref, lower_ref, upper_ref, order_ref, lists_ref,
    ) = held
    (
        hout, hin, tile_out, tile_in, c_out, c_in, a_in, coef_in, perm, schur, neumann, half, vbuf, wide, wide_t, inner, turned,
        share, diag, mean, own_w, near_w, x, r, p, image, totals, moved,
        hs, hr, ts, tr, cs, cr, as_, ar, fs, fr,
    ) = refs
    k = lax.axis_index("axial")
    c = lax.axis_index("circ")
    width = perm.shape[1]
    arrivals = [
        pltpu.make_async_copy(source, target, in_sem.at[i])
        for i, (source, target) in enumerate(zip(sources, held))
    ]
    for i in (9, 1, 2, 10, 0, 7, 8, 6, 5, 3, 4):
        arrivals[i].start()
    block = blocks_ref.shape[-1]
    list_len = lists_ref.shape[-1]

    def circ_peer(d):
        return {"circ": lax.rem(c + d, cols)}

    def axial_peer(d):
        return {"axial": lax.rem(k + d, rows)}

    barrier = pltpu.get_barrier_semaphore()
    for d in range(1, cols):
        pl.semaphore_signal(barrier, inc=1, device_id=circ_peer(d), device_id_type=MESH)
    for d in range(1, rows):
        pl.semaphore_signal(barrier, inc=1, device_id=axial_peer(d), device_id_type=MESH)

    has = (k > 0, k < rows - 1)
    keep = [has[0].astype(F32), has[1].astype(F32)]

    def across(f):
        if f == 0:
            return {"axial": jnp.maximum(k - 1, 0)}
        if f == 1:
            return {"axial": jnp.minimum(k + 1, rows - 1)}
        return {"circ": lax.rem(c + (cols - 1 if f == 2 else 1), cols)}

    def face_copy(out, into, send, recv, t, f):
        return pltpu.make_async_remote_copy(
            src_ref=out.at[t, f],
            dst_ref=into.at[t, f ^ 1],
            send_sem=send.at[t, f],
            recv_sem=recv.at[t, f ^ 1],
            device_id=across(f),
            device_id_type=MESH,
        )

    def guarded(f, action):
        if f < 2:
            pl.when(has[f])(action)
        else:
            action()

    def send_face(args, t, f):
        guarded(f, lambda: face_copy(*args, t, f).start())

    def wait_face(args, t, f):
        guarded(f, lambda: face_copy(*args, t, f ^ 1).wait_recv())

    def done_face(args, t, f):
        guarded(f, lambda: face_copy(*args, t, f).wait_send())

    halo = (hout, hin, hs, hr)
    tiles = (tile_out, tile_in, ts, tr)

    for f in range(2):

        @pl.when(jnp.logical_not(has[f]))
        def _():
            tile_in[0, f] = jnp.zeros(tile_in.shape[2:], F32)
            for t in range(HALOS):
                hin[t, f] = jnp.zeros(hin.shape[2:], F32)

    sub = lax.broadcasted_iota(jnp.int32, (width, width), 0)
    lane = lax.broadcasted_iota(jnp.int32, (width, width), 1)
    list_sub = lax.broadcasted_iota(jnp.int32, (width, list_len), 0)

    def spread(column):
        return jnp.broadcast_to(column, (width, width))

    for i in (9, 1, 2, 10, 0):
        arrivals[i].wait()

    wide[...] = jnp.zeros_like(wide)
    wide_t[...] = jnp.zeros_like(wide_t)
    inner[...] = jnp.zeros_like(inner)

    for f in range(4):
        span = pl.ds(f * width, width)
        one = (order_ref[0, :, span] - f * width == sub).astype(F32)
        perm[f] = one.astype(BF16)
        corner = pl.ds((f % 2) * width, width)
        wide[f // 2, corner, corner] = one.astype(BF16)
        wide_t[f // 2, corner, corner] = one.T.astype(BF16)
        rho = jnp.sum(one * rho_ref[0, :, span], axis=1, keepdims=True)
        dia = jnp.sum(one * diag_ref[0, :, span], axis=1, keepdims=True)
        diag[f] = spread(dia)
        share[f] = spread(rho)
        member = []
        for i in range(2):
            named = (lists_ref[0, 0, pl.ds(2 * f + i, 1), :] - f * width == list_sub).astype(F32)
            member.append(jnp.sum(named, axis=1, keepdims=True))
        pair = jnp.where(lane == 0, member[0], jnp.where(lane == 1, member[1], 0.0))
        pair = dot16(one.astype(BF16), pair.astype(BF16)) / list_len
        mean[2 * f] = spread(pair[:, 0:1])
        mean[2 * f + 1] = spread(pair[:, 1:2])
        packed = jnp.where(
            lane == 0, rho, jnp.where(lane == 1, pair[:, 0:1], jnp.where(lane == 2, pair[:, 1:2], 0.0))
        )
        tile_out[0, f] = packed.T[0:8]
        full = dot16(perm[f], jnp.concatenate(split3(load_ref[0, 0, :, span].T), axis=1))
        tail = full[:, width : 2 * width] + full[:, 2 * width :]
        hout[0, f] = full[:, :width] + tail

    pl.semaphore_wait(barrier, rows + cols - 2)
    for f in (2, 3, 0, 1):
        send_face(tiles, 0, f)
    for f in (2, 3, 0, 1):
        send_face(halo, 0, f)

    for i in (7, 8, 6):
        arrivals[i].wait()

    small_sub = lax.broadcasted_iota(jnp.int32, (8, 8), 0)
    small_lane = lax.broadcasted_iota(jnp.int32, (8, 8), 1)
    for i, ref in enumerate((lower_ref, upper_ref)):
        column = jnp.sum(jnp.where(small_sub == small_lane, ref[...], 0.0), axis=1, keepdims=True)
        coef_in[k, i] = jnp.broadcast_to(column, (8, width))

    def coef_copy(d):
        return pltpu.make_async_remote_copy(
            src_ref=coef_in.at[k],
            dst_ref=coef_in.at[k],
            send_sem=fs.at[d],
            recv_sem=fr.at[d],
            device_id=axial_peer(d),
            device_id_type=MESH,
        )

    def coef_arrival(d):
        row = lax.rem(k + rows - d, rows)
        return pltpu.make_async_remote_copy(
            src_ref=coef_in.at[row],
            dst_ref=coef_in.at[row],
            send_sem=fs.at[d],
            recv_sem=fr.at[d],
            device_id=axial_peer(d),
            device_id_type=MESH,
        )

    for d in range(1, rows):
        coef_copy(d).start()

    for f in (0, 1, 2, 3):
        wait_face(tiles, 0, f)
        got = jnp.concatenate([tile_in[0, f], jnp.zeros((width - 8, width), F32)], axis=0).T
        mine = share[f]
        theirs = spread(got[:, 0:1])
        both = mine + theirs
        own_share = mine / both
        near_share = theirs / both
        share[f] = own_share
        masked = own_share * keep[f] if f < 2 else own_share
        for i in range(2):
            own_w[2 * f + i] = masked * mean[2 * f + i]
            near_w[2 * f + i] = near_share * spread(got[:, 1 + i : 2 + i])

    def span_of(t):
        return pl.ds(8, 8) if t == ITERS else pl.ds(0, 16)

    def circ_copy(t, d):
        return pltpu.make_async_remote_copy(
            src_ref=c_out.at[t, span_of(t)],
            dst_ref=c_in.at[t, d, span_of(t)],
            send_sem=cs.at[t, d],
            recv_sem=cr.at[t, d],
            device_id=circ_peer(d),
            device_id_type=MESH,
        )

    def axial_copy(t, d, row):
        return pltpu.make_async_remote_copy(
            src_ref=a_in.at[t, row, span_of(t)],
            dst_ref=a_in.at[t, row, span_of(t)],
            send_sem=as_.at[t, d],
            recv_sem=ar.at[t, d],
            device_id=axial_peer(d),
            device_id_type=MESH,
        )

    def sum_begin(t, value):
        c_out[t, span_of(t)] = value
        for d in range(1, cols):
            circ_copy(t, d).start()

    def sum_middle(t):
        value = c_out[t, span_of(t)]
        for d in range(1, cols):
            circ_copy(t, d).wait_recv()
            value = value + c_in[t, d, span_of(t)]
        a_in[t, k, span_of(t)] = value
        for d in range(1, rows):
            axial_copy(t, d, k).start()

    def sum_end(t):
        for d in range(1, rows):
            axial_copy(t, d, lax.rem(k + rows - d, rows)).wait_recv()

    def dot_total(t, row):
        value = a_in[t, 0, pl.ds(row, 1)]
        for m in range(1, rows):
            value = value + a_in[t, m, pl.ds(row, 1)]
        return value

    sub8 = lax.broadcasted_iota(jnp.int32, (8, width), 0)

    def dot_tile(dots, head):
        dots = dots + [jnp.zeros((1, width), F32)] * (4 - len(dots))
        return jnp.concatenate(head + dots, axis=0)

    def constraint_tiles(field, dots):
        def one(table, index, f):
            return jnp.sum(table[index] * field(f), axis=0, keepdims=True)

        first = []
        for q in range(8):
            value = own_w[q] * field(q // 2)
            if q in (4, 5):
                value = value + near_w[q + 2] * field(3)
            if q in (6, 7):
                value = value + near_w[q - 2] * field(2)
            first.append(jnp.sum(value, axis=0, keepdims=True))
        second = [one(near_w, 2, 1), one(near_w, 3, 1), one(near_w, 0, 0), one(near_w, 1, 0)]
        return dot_tile(dots, first + second)

    def row_totals(t, m):
        value = a_in[t, m, pl.ds(0, 8)]
        if m > 0:
            value = value + jnp.where(sub8 < 2, a_in[t, m - 1, pl.ds(8, 8)], 0.0)
        if m < rows - 1:
            value = value + jnp.where(
                jnp.logical_and(sub8 >= 2, sub8 < 4), a_in[t, m + 1, pl.ds(8, 8)], 0.0
            )
        return value

    sum_begin(0, constraint_tiles(lambda f: hout[0, f], []))

    arrivals[5].wait()

    def store_pair(table, f, cut, value):
        high, low = split(value)
        table[f, pl.ds(0, width), cut] = high
        table[f, pl.ds(width, width), cut] = low

    points = 4 * width
    pair = 2 * width
    high, low = split(neumann_ref[0, 0])
    for a in range(2):
        cut = slice(a * pair, (a + 1) * pair)
        for i, part in enumerate((high, low)):
            turned[pl.ds(i * points, points), pl.ds(a * pair, pair)] = dot16(
                part[:, cut], wide_t[a]
            ).astype(BF16)
    for a in range(2):
        for i in range(2):
            done = dot16(wide[a], turned[pl.ds(i * points + a * pair, pair), :]).astype(BF16)
            for j in range(2):
                neumann[2 * a + j, pl.ds(i * width, width), :] = done[j * width : (j + 1) * width]

    sum_middle(0)

    def apply(table, field):
        for f in range(4):
            high, low = split(field(f))
            vbuf[pl.ds(f * width, width), pl.ds(0, width)] = high
            vbuf[pl.ds(f * width, width), pl.ds(width, width)] = low

        def one(f):
            full = dot16(table[f], vbuf[...])
            small = full[:width, width:] + full[width:, :width] + full[width:, width:]
            return full[:width, :width] + small

        return one

    def assembled(t, f):
        value = hout[t, f] + hin[t, f]
        return value * keep[f] if f < 2 else value

    def coarse_value():
        smooth = []
        h = jnp.zeros((8, width), F32)
        for m in range(rows):
            factor = coef_in[m, 0]
            h = factor * h + (1.0 - factor) * totals[m]
            smooth.append(h)
        top = jnp.zeros((8, width), F32)
        mine = jnp.zeros((8, width), F32)
        for m in reversed(range(rows)):
            factor = coef_in[m, 1]
            top = factor * top + (1.0 - factor) * smooth[m]
            mine = mine + jnp.where(k == m, top, 0.0)
        own = totals[k]
        for q in range(8):
            mine = mine + coarse_ref[0, :, pl.ds(q, 1)] * own[q : q + 1]
        return mine

    def precondition(t):
        local = apply(neumann, lambda f: share[f] * r[f])
        coarse = coarse_value()
        for f in (2, 3, 0, 1):
            value = local(f)
            for i in range(2):
                q = 2 * f + i
                value = value + mean[q] * coarse[q : q + 1]
            value = share[f] * value
            hout[t, f] = value
            send_face(halo, t, f)

    for f in (0, 1, 2, 3):
        wait_face(halo, 0, f)
        r[f] = assembled(0, f)
    sum_end(0)
    for d in range(1, rows):
        coef_arrival(d).wait_recv()
    for m in range(rows):
        totals[m] = row_totals(0, m)
    precondition(1)

    arrivals[3].wait()
    arrivals[4].wait()

    high, low = split(couple_ref[0, 0])
    for a in range(2):
        cut = slice(a * pair, (a + 1) * pair)
        for i, part in enumerate((high, low)):
            half[i, pl.ds(a * pair, pair), :] = dot16(wide[a], part[cut]).astype(BF16)
    for n in range(blocks_ref.shape[2]):
        corner = pl.ds((n % 2) * block, block)
        for i, part in enumerate(split(blocks_ref[0, 0, n])):
            inner[i, n // 2, corner, corner] = part
    for a in range(2):
        cut = pl.ds(a * pair, pair)
        ch, cl = half[0, :, cut], half[1, :, cut]
        ih, il = inner[0, a], inner[1, a]
        high, low = split(dot16(ch, ih) + (dot16(ch, il) + dot16(cl, ih)))
        half[2, :, cut] = high
        half[3, :, cut] = low
    both = dot16(half[pl.ds(2, 2)].reshape(2 * points, points), half[0], NT)
    value = both[:points] + (both[points:] + dot16(half[2], half[1], NT))
    for f in range(4):
        store_pair(schur, f, slice(None), value[f * width : (f + 1) * width])

    def fold(value):
        return jnp.sum(value, axis=0, keepdims=True)

    rz = None
    pap = None
    for step in range(ITERS):
        t = 1 + 2 * step
        last = step + 1 == ITERS
        for f in (0, 1, 2, 3):
            wait_face(halo, t, f)
        back = apply(schur, lambda f: assembled(t, f))
        dots = [jnp.zeros((1, width), F32) for _ in range(2 if step == 0 else 3)]
        for f in (2, 3, 0, 1):
            z = assembled(t, f)
            value = diag[f] * z - back(f)
            hout[t + 1, f] = value
            dots[0] = dots[0] + 0.5 * fold(r[f] * z)
            dots[1] = dots[1] + fold(z * value)
            if step > 0:
                dots[2] = dots[2] + fold(0.5 * (z * image[f]) + p[f] * value)
        if last:
            sum_begin(step + 1, dot_tile(dots, [jnp.zeros((1, width), F32)] * 4))
        else:
            sum_begin(step + 1, constraint_tiles(lambda f: hout[t + 1, f], dots))
        for f in (2, 3):
            send_face(halo, t + 1, f)
        sum_middle(step + 1)
        for f in (0, 1):
            send_face(halo, t + 1, f)
        for f in (0, 1, 2, 3):
            wait_face(halo, t + 1, f)
        sum_end(step + 1)
        new = dot_total(step + 1, 12)
        new_pap = dot_total(step + 1, 13)
        if step > 0:
            beta = new / rz
            new_pap = new_pap + beta * (dot_total(step + 1, 14) + beta * pap)
        rz, pap = new, new_pap
        alpha = rz / pap
        for f in range(4):
            z = assembled(t, f)
            w = assembled(t + 1, f)
            if step > 0:
                z = z + beta * p[f]
                w = w + beta * image[f]
            p[f] = z
            image[f] = w
            x[f] = alpha * z if step == 0 else x[f] + alpha * z
            r[f] = r[f] - alpha * w
        if not last:
            for m in range(rows):
                value = row_totals(step + 1, m)
                if step > 0:
                    value = value + beta * moved[m]
                moved[m] = value
                totals[m] = totals[m] - alpha * value
            precondition(t + 2)

    for f in range(4):
        span = pl.ds(f * width, width)
        parts = split3(x[f].T) + split3(r[f].T)
        full = dot16(jnp.concatenate(parts, axis=0), perm[f])
        full = [full[i * width : (i + 1) * width] for i in range(6)]
        x_out[0, 0, :, span] = full[0] + (full[1] + full[2])
        r_out[0, 0, :, span] = full[3] + (full[4] + full[5])

    for f in range(4):
        done_face(tiles, 0, f)
        for t in range(HALOS):
            done_face(halo, t, f)
    for d in range(1, rows):
        coef_copy(d).wait_send()
    for t in range(SUMS):
        for d in range(1, cols):
            circ_copy(t, d).wait_send()
        for d in range(1, rows):
            axial_copy(t, d, k).wait_send()


def local(rows, cols, *args):
    load = args[0]
    count, points = load.shape[2:]
    width = points // 4
    dma = pltpu.SemaphoreType.DMA
    face = (4, width, width)
    scratch = [pltpu.VMEM(arg.shape, arg.dtype) for arg in args] + [
        dma((len(args),)),
        pltpu.VMEM((HALOS,) + face, F32),
        pltpu.VMEM((HALOS,) + face, F32),
        pltpu.VMEM((1, 4, 8, width), F32),
        pltpu.VMEM((1, 4, 8, width), F32),
        pltpu.VMEM((SUMS, 16, width), F32),
        pltpu.VMEM((SUMS, cols, 16, width), F32),
        pltpu.VMEM((SUMS, rows, 16, width), F32),
        pltpu.VMEM((rows, 2, 8, width), F32),
        pltpu.VMEM(face, BF16),
        pltpu.VMEM((4, 2 * width, points), BF16),
        pltpu.VMEM((4, 2 * width, points), BF16),
        pltpu.VMEM((4, points, args[3].shape[-1]), BF16),
        pltpu.VMEM((points, 2 * width), BF16),
        pltpu.VMEM((2, 2 * width, 2 * width), BF16),
        pltpu.VMEM((2, 2 * width, 2 * width), BF16),
        pltpu.VMEM((2, 2, 2 * width, 2 * width), BF16),
        pltpu.VMEM((2 * points, points), BF16),
        pltpu.VMEM(face, F32),
        pltpu.VMEM(face, F32),
        pltpu.VMEM((8, width, width), F32),
        pltpu.VMEM((8, width, width), F32),
        pltpu.VMEM((8, width, width), F32),
        pltpu.VMEM(face, F32),
        pltpu.VMEM(face, F32),
        pltpu.VMEM(face, F32),
        pltpu.VMEM(face, F32),
        pltpu.VMEM((rows, 8, width), F32),
        pltpu.VMEM((rows, 8, width), F32),
        dma((HALOS, 4)),
        dma((HALOS, 4)),
        dma((1, 4)),
        dma((1, 4)),
        dma((SUMS, cols)),
        dma((SUMS, cols)),
        dma((SUMS, rows)),
        dma((SUMS, rows)),
        dma((rows,)),
        dma((rows,)),
    ]
    shape = jax.ShapeDtypeStruct(load.shape, F32)
    return pl.pallas_call(
        functools.partial(kernel, rows, cols),
        out_shape=(shape, shape),
        in_specs=[pl.BlockSpec(memory_space=pl.ANY)] * len(args),
        out_specs=(pl.BlockSpec(memory_space=pltpu.VMEM),) * 2,
        scratch_shapes=scratch,
        compiler_params=pltpu.CompilerParams(
            collective_id=0, has_side_effects=True, vmem_limit_bytes=56 * 2**20
        ),
    )(*args)


def solution(mesh):
    in_specs = (
        P("axial", "circ", None, None),
        P("axial", "circ", None),
        P("axial", "circ", None),
        P("axial", "circ", None, None),
        P("axial", "circ", None, None, None),
        P("axial", "circ", None, None),
        P("axial", None, None),
        P("axial", None),
        P("axial", None),
        P("axial", "circ", None),
        P("axial", "circ", None, None),
    )
    out_specs = (P("axial", "circ", None, None), P("axial", "circ", None, None))
    body = functools.partial(local, mesh.shape["axial"], mesh.shape["circ"])
    return jax.shard_map(body, mesh=mesh, in_specs=in_specs, out_specs=out_specs, check_vma=False)
```
